32 devices in a mesh: dp: 8 (over z, x), seq: 4 (over y, core).
Axes of the slice: x: 2, y: 2, z: 4, core: 2. Of those that a mesh axis runs over, the one named last changes fastest.
Arguments:
- tokens: bfloat16 [16, 512, 2048], P('dp', 'seq'), may hold values from -6 to 6
- segments: int32 [16, 512], P('dp'), may hold values from 0 to 2, as said below
- cotangent: bfloat16 [16, 512, 2048], P('dp', 'seq'), may hold values from -6 to 6
- w_query: bfloat16 [2048, 2048], P(('dp', 'seq')), may hold values from -0.125 to 0.125
- key_projection_weight: bfloat16 [2048, 1024], P(('dp', 'seq')), may hold values from -0.125 to 0.125
- value_projection_weight: bfloat16 [2048, 1024], P(('dp', 'seq')), may hold values from -0.125 to 0.125
- w_output: bfloat16 [2048, 2048], P(('dp', 'seq')), may hold values from -1.5 to 1.5
- w_gate: bfloat16 [2048, 6144], P(('dp', 'seq')), may hold values from -0.125 to 0.125
- w_up: bfloat16 [2048, 6144], P(('dp', 'seq')), may hold values from -0.125 to 0.125
- w_down: bfloat16 [6144, 2048], P(('dp', 'seq')), may hold values from -0.078125 to 0.078125
- gain_attn: bfloat16 [2048], P(('dp', 'seq')), may hold values from 0.5 to 1.5
- gain_query: bfloat16 [128], P(('dp', 'seq')), may hold values from 0.5 to 1.5
- gain_key: bfloat16 [128], P(('dp', 'seq')), may hold values from 0.5 to 1.5
- gain_mlp: bfloat16 [2048], P(('dp', 'seq')), may hold values from 0.5 to 1.5
Outputs:
- layer_out: bfloat16 [16, 512, 2048], P('dp', 'seq')
- input_grad: bfloat16 [16, 512, 2048], P('dp', 'seq')
- query_wgrad: float32 [2048, 2048], P(('dp', 'seq'))
- key_wgrad: float32 [2048, 1024], P(('dp', 'seq'))
- value_wgrad: float32 [2048, 1024], P(('dp', 'seq'))
- output_wgrad: float32 [2048, 2048], P(('dp', 'seq'))
- gate_wgrad: float32 [2048, 6144], P(('dp', 'seq'))
- up_wgrad: float32 [2048, 6144], P(('dp', 'seq'))
- down_wgrad: float32 [6144, 2048], P(('dp', 'seq'))
- attn_gain_grad: float32 [2048], P(('dp', 'seq'))
- query_gain_grad: float32 [128], P(('dp', 'seq'))
- key_gain_grad: float32 [128], P(('dp', 'seq'))
- mlp_gain_grad: float32 [2048], P(('dp', 'seq'))
The draws below stay inside these ranges and needn't reach their ends.
Inputs may be any that keep to these rules, and one draw needn't show every extreme that they name: `segments`: within a sequence the numbers never fall; each sequence holds three documents: document 1 has tokens among the first 128 and among the last 128 of its sequence, and documents 0 and 2 are the cut-off ends of documents packed across the sequence's bounds.
All inputs are finite; a program needn't handle non-finite values.
Results may differ from the reference program's by a relative error of at most 0.015.
Values may be sent and summed in bfloat16 or wider, within the bound.
No kernel may reach another device: no remote copies, remote signals or barrier semaphores. Data moves between devices by JAX's collectives and lax.ppermute only.
A program may use at most 448 MiB of HBM per device.

```python
import jax
import jax.numpy as jnp
from jax import lax

MODEL_WIDTH = 2048
HQ = 16
KEY_VALUE_HEADS = 8
HEAD_DIM = 128
FF = 6144
SEQ_LEN = 512
SHARD = 128
SEQUENCES = 16


def draw_segments(key, part):
    key = jax.random.fold_in(key, 7)
    first_key, second_key = jax.random.split(key)
    starts = jax.random.randint(first_key, (SEQUENCES, 1), SHARD // 4, SHARD)
    finishes = jax.random.randint(second_key, (SEQUENCES, 1), SEQ_LEN - SHARD + 1, SEQ_LEN - SHARD // 4 + 1)
    indices = jnp.arange(SEQ_LEN, dtype=jnp.int32)[None, :]
    return (indices >= starts).astype(jnp.int32) + (indices >= finishes).astype(jnp.int32)


def raised(values, stream_key, source, target, blocks, factor):
    def block_of(dim):
        return (jnp.arange(values.shape[dim]) // (values.shape[dim] // blocks)).reshape((-1,) + (1,) * (values.ndim - 1 - dim))

    one_side = jax.random.permutation(stream_key, blocks)[block_of(target)]
    second = (block_of(target) + blocks // 2) % blocks
    return jnp.where((block_of(source) == one_side) | (block_of(source) == second), factor * values, values)


def block_levels(rng, extent, shards, smallest, largest):
    factor_of, own = 1.0, jax.random.fold_in(rng, 6)
    for axis_at, parts in shards:
        heights = jnp.exp(jax.random.uniform(jax.random.fold_in(own, axis_at), (parts,), jnp.float32, smallest / len(shards), largest / len(shards)))
        factor_of = factor_of * jnp.repeat(heights, extent[axis_at] // parts).reshape([-1 if axis == axis_at else 1 for axis in range(len(extent))])
    return factor_of


def bell_draw(own_key, extent, spread, reach, cuts=(), held_as=jnp.bfloat16):
    factor_of = block_levels(own_key, extent, cuts, -0.22, 0.18) if cuts else 1.0
    array = jax.random.normal(own_key, extent, jnp.float32) * spread * factor_of
    return jnp.minimum(jnp.maximum(array, -reach), reach).astype(held_as)


def heavy_noise(rng, shape, width, bound, cuts, heavy, held_as=jnp.bfloat16):
    entries = width * jax.random.normal(rng, shape, jnp.float32)
    if cuts:
        entries = entries * block_levels(rng, shape, cuts, -0.22, 0.18)
    return jnp.clip(raised(entries, jax.random.fold_in(rng, 3), *heavy), -bound, bound).astype(held_as)


def setup_inputs(seed: int = 0) -> dict:
    keys = jax.random.split(jax.random.key(seed), 15)
    return {
        "tokens": heavy_noise(keys[0], (SEQUENCES, SEQ_LEN, MODEL_WIDTH), 1.0, 6.0, ((0, 8), (1, 4)), (0, 2, 8, 2.0)),
        "segments": draw_segments(jax.random.fold_in(keys[14], 71), 0),
        "cotangent": bell_draw(keys[2], (SEQUENCES, SEQ_LEN, MODEL_WIDTH), 1.0, 6.0, ((0, 8), (1, 4))),
        "w_query": bell_draw(keys[3], (MODEL_WIDTH, HQ * HEAD_DIM), MODEL_WIDTH ** -0.5, 0.125, ((0, 32),)),
        "key_projection_weight": bell_draw(keys[4], (MODEL_WIDTH, KEY_VALUE_HEADS * HEAD_DIM), MODEL_WIDTH ** -0.5, 0.125, ((0, 32),)),
        "value_projection_weight": bell_draw(keys[5], (MODEL_WIDTH, KEY_VALUE_HEADS * HEAD_DIM), MODEL_WIDTH ** -0.5, 0.125, ((0, 32),)),
        "w_output": bell_draw(keys[6], (HQ * HEAD_DIM, MODEL_WIDTH), (HQ * HEAD_DIM // 128) ** -0.5, 1.5, ((0, 32),)),
        "w_gate": bell_draw(keys[7], (MODEL_WIDTH, FF), MODEL_WIDTH ** -0.5, 0.125, ((0, 32),)),
        "w_up": bell_draw(keys[8], (MODEL_WIDTH, FF), MODEL_WIDTH ** -0.5, 0.125, ((0, 32),)),
        "w_down": bell_draw(keys[9], (FF, MODEL_WIDTH), FF ** -0.5, 0.078125, ((0, 32),)),
        "gain_attn": jnp.clip(1.0 + 0.1 * jax.random.normal(keys[10], (MODEL_WIDTH,), jnp.float32), 0.5, 1.5).astype(jnp.bfloat16),
        "gain_query": jnp.clip(1.0 + 0.1 * jax.random.normal(keys[11], (HEAD_DIM,), jnp.float32), 0.5, 1.5).astype(jnp.bfloat16),
        "gain_key": jnp.clip(1.0 + 0.1 * jax.random.normal(keys[12], (HEAD_DIM,), jnp.float32), 0.5, 1.5).astype(jnp.bfloat16),
        "gain_mlp": jnp.clip(1.0 + 0.1 * jax.random.normal(keys[13], (MODEL_WIDTH,), jnp.float32), 0.5, 1.5).astype(jnp.bfloat16),
    }


EPSILON = 1e-06
THETA = 1000000.0
HIGHEST = lax.Precision.HIGHEST

@jax.custom_vjp
def low(v):
    return lax.optimization_barrier(v.astype(jnp.bfloat16)).astype(jnp.float32)

@jax.custom_vjp
def low_back(v):
    return v

def low_keep(v):
    return (low(v), None)

def low_pass(kept, grad):
    return (grad,)

def back_keep(v):
    return (v, None)

def back_low(kept, grad):
    return (low(grad),)
low.defvjp(low_keep, low_pass)
low_back.defvjp(back_keep, back_low)

def rms_norm(values, gain):
    return values * lax.rsqrt(lax.optimization_barrier(jnp.mean(values * values, axis=-1, keepdims=True)) + EPSILON) * gain

def rope_tables(positions, head_size):
    half_size = head_size // 2
    frequency = jnp.power(THETA, -(jnp.arange(half_size, dtype=jnp.float32) * 2.0 / head_size))
    angles = positions[..., None] * frequency
    cosine = jnp.concatenate([jnp.cos(angles), jnp.cos(angles)], axis=-1)[..., None, :]
    sine_table = jnp.concatenate([jnp.sin(angles), jnp.sin(angles)], axis=-1)[..., None, :]
    return (cosine, sine_table)

def rotate(values, cosine, sine_table):
    half_size = values.shape[-1] // 2
    turned = jnp.concatenate([-values[..., half_size:], values[..., :half_size]], axis=-1)
    return values * cosine + turned * sine_table

def matmul(left, right):
    return jnp.dot(left, right, precision=HIGHEST)

def layer(inputs, segment_row, w_query, key_projection_weight, value_projection_weight, w_output, w_gate, w_up, w_down, gain_attn, gain_query, gain_key, gain_mlp):
    length = inputs.shape[0]
    head_size = gain_query.shape[0]
    indices = jnp.arange(length, dtype=jnp.int32)
    same_doc = segment_row[:, None] == segment_row[None, :]
    visible = same_doc & (indices[None, :] <= indices[:, None])
    doc_start = lax.optimization_barrier(jnp.min(jnp.where(same_doc, indices[None, :], length), axis=-1))
    positions = (indices - doc_start).astype(jnp.float32)
    cosine, sine_table = rope_tables(positions, head_size)
    normed = low(rms_norm(inputs, gain_attn))
    query_projected = low_back(matmul(normed, w_query)).reshape(length, -1, head_size)
    key_projected = low_back(matmul(normed, key_projection_weight)).reshape(length, -1, head_size)
    value_reduced = low(low_back(matmul(normed, value_projection_weight))).reshape(length, -1, head_size)
    query_rot = low(rotate(rms_norm(query_projected, gain_query), cosine, sine_table))
    key_rot = low(rotate(rms_norm(key_projected, gain_key), cosine, sine_table))
    kv_heads = key_rot.shape[1]
    query_four = query_rot.reshape(length, kv_heads, -1, head_size)
    raw_scores = low_back(jnp.einsum('qkgd,pkd->kgqp', query_four, key_rot, precision=HIGHEST) * head_size ** (-0.5))
    masked = jnp.where(visible[None, None], raw_scores, -1e+30)
    row_max = lax.optimization_barrier(jnp.max(masked, axis=-1, keepdims=True))
    exponent = jnp.exp(masked - row_max)
    probs = low(exponent / lax.optimization_barrier(jnp.sum(exponent, axis=-1, keepdims=True)))
    mixed_rows = jnp.einsum('kgqp,pkd->qkgd', probs, value_reduced, precision=HIGHEST).reshape(length, -1)
    mixed_rows = low(low_back(mixed_rows))
    middle = inputs + low_back(matmul(mixed_rows, w_output))
    normed_two = low(rms_norm(middle, gain_mlp))
    gate_rows = low_back(matmul(normed_two, w_gate))
    up_projected = low_back(matmul(normed_two, w_up))
    hidden_rows = low(jax.nn.silu(gate_rows) * up_projected)
    return middle + low_back(matmul(hidden_rows, w_down))

def reference(tokens, segments, cotangent, w_query, key_projection_weight, value_projection_weight, w_output, w_gate, w_up, w_down, gain_attn, gain_query, gain_key, gain_mlp):
    params = tuple((w.astype(jnp.float32) for w in (w_query, key_projection_weight, value_projection_weight, w_output, w_gate, w_up, w_down, gain_attn, gain_query, gain_key, gain_mlp)))

    def one_sequence(totals, item):
        inputs, segment_row, out_grad = item

        def forward(values, *weights):
            return layer(values, segment_row, *weights)
        result, pullback = jax.vjp(forward, inputs.astype(jnp.float32), *params)
        gradients = pullback(out_grad.astype(jnp.float32))
        totals = tuple((total + grad_part for total, grad_part in zip(totals, gradients[1:])))
        return (totals, (result.astype(jnp.bfloat16), gradients[0].astype(jnp.bfloat16)))
    initial = tuple((jnp.zeros(w.shape, jnp.float32) for w in params))
    totals, (outputs, in_grads) = lax.scan(one_sequence, initial, (tokens, segments, cotangent))
    return (outputs, in_grads, totals[0], totals[1], totals[2], totals[3], totals[4], totals[5], totals[6], totals[7], totals[8], totals[9], totals[10])
```

```python
import jax
import jax.numpy as jnp
from jax import lax
from jax.experimental import pallas as pl
from jax.experimental.pallas import tpu as pltpu
from jax.sharding import Mesh
from jax.sharding import PartitionSpec as P

EPSILON = 1e-06
THETA = 1000000.0
PLANE = ("inner", "seq")
EVERY = ("outer", "inner", "seq")
BF16 = jnp.bfloat16
F32 = jnp.float32
VMEM_LIMIT = 56 * 1024 * 1024


def rms_scale(values):
    return lax.rsqrt(jnp.mean(values * values, axis=-1, keepdims=True) + EPSILON)


def norm_back(normalized_grad, normalized, inverse_rms):
    return inverse_rms * (
        normalized_grad
        - normalized * jnp.mean(normalized_grad * normalized, axis=-1, keepdims=True)
    )


def plane_routes(outer):
    def pairs(flip):
        out = []
        for o in range(outer):
            for x in range(2):
                for y in range(2):
                    for c in range(2):
                        fx, fy, fc = flip(c)
                        source = ((o * 2 + x) * 2 + y) * 2 + c
                        target = ((o * 2 + (x ^ fx)) * 2 + (y ^ fy)) * 2 + (c ^ fc)
                        out.append((source, target))
        return out

    return (
        pairs(lambda c: (1, 0, 0) if c == 0 else (0, 1, 0)),
        pairs(lambda c: (0, 1, 0) if c == 0 else (1, 0, 0)),
        pairs(lambda c: (0, 0, 1)),
        pairs(lambda c: (1, 0, 0)),
    )


def plane_gather(block, routes, first_core):
    route_a, route_b, route_c, _ = routes
    near_a = lax.ppermute(block, EVERY, route_a)
    near_b = lax.ppermute(block, EVERY, route_b)
    far = lax.ppermute(near_a, EVERY, route_b)
    half = jnp.stack(
        [
            block,
            jnp.where(first_core, near_b, near_a),
            jnp.where(first_core, near_a, near_b),
            far,
        ]
    )
    other = lax.ppermute(half, EVERY, route_c)
    return jnp.concatenate([half, other], axis=0)


def plane_scatter(blocks, routes, first_core):
    route_a, route_b, route_c, _ = routes
    arrived = lax.ppermute(blocks[4:], EVERY, route_c)
    total = blocks[:4].astype(F32) + arrived.astype(F32)
    near_a = jnp.where(first_core, total[2], total[1])
    near_b = jnp.where(first_core, total[1], total[2]).astype(BF16)
    far = lax.ppermute(total[3].astype(BF16), EVERY, route_b)
    from_b = lax.ppermute(near_b, EVERY, route_b)
    from_a = lax.ppermute((near_a + far.astype(F32)).astype(BF16), EVERY, route_a)
    return total[0] + from_b.astype(F32) + from_a.astype(F32)


def turn(values):
    return pltpu.roll(values, values.shape[-1] // 2, 1)


def head_forward(projected, gain, cosine, sine):
    scale = rms_scale(projected)
    hat = projected * scale
    scaled = hat * gain
    return scale, hat, (scaled * cosine + turn(scaled) * sine).astype(BF16)


def head_backward(rotated_grad, gain, scale, hat, cosine, sine):
    grad = rotated_grad * cosine - turn(rotated_grad) * sine
    gain_grad = jnp.sum(grad * hat, axis=0, keepdims=True)
    return gain_grad, norm_back(grad * gain, hat, scale).astype(BF16)


def matmul(left, right, dims):
    return lax.dot_general(left, right, (dims, ((), ())), preferred_element_type=F32)


def head_probs(query_rot, key_rot, visible):
    head_size = query_rot.shape[-1]
    raw = matmul(query_rot, key_rot, ((1,), (1,))) * head_size ** (-0.5)
    masked = jnp.where(visible, raw, -1e30)
    exponent = jnp.exp(masked - jnp.max(masked, axis=-1, keepdims=True))
    return exponent / jnp.sum(exponent, axis=-1, keepdims=True)


def visibility(index_row_ref, index_col_ref, start_ref):
    index_row = index_row_ref[...]
    return (index_row >= start_ref[...]) & (index_row <= index_col_ref[...])


def attention_kernel(
    projected_ref, cosine_ref, sine_ref, start_ref, index_col_ref, index_row_ref, gain_ref, mixed_ref
):
    head_size = cosine_ref.shape[-1]
    length = cosine_ref.shape[0]
    groups = mixed_ref.shape[-1] // head_size
    cosine, sine = (cosine_ref[...], sine_ref[...])
    visible = visibility(index_row_ref, index_col_ref, start_ref)
    projected = projected_ref[...].reshape(length, -1)
    gain_query, gain_key = (gain_ref[0:1], gain_ref[1:2])
    key_at = groups * head_size
    _, _, key_rot = head_forward(
        projected[:, key_at : key_at + head_size], gain_key, cosine, sine
    )
    value = projected[:, key_at + head_size :].astype(BF16)
    for head in range(groups):
        columns = slice(head * head_size, (head + 1) * head_size)
        _, _, query_rot = head_forward(projected[:, columns], gain_query, cosine, sine)
        probs = head_probs(query_rot, key_rot, visible).astype(BF16)
        mixed = matmul(probs, value, ((1,), (0,))).astype(BF16)
        mixed_ref[..., columns] = mixed.reshape(mixed_ref.shape[:-1] + (head_size,))


def attention_back_kernel(
    projected_ref,
    mixed_grad_ref,
    cosine_ref,
    sine_ref,
    start_ref,
    index_col_ref,
    index_row_ref,
    gain_ref,
    low_ref,
    gain_grad_ref,
):
    head_size = cosine_ref.shape[-1]
    length = cosine_ref.shape[0]
    groups = mixed_grad_ref.shape[-1] // head_size
    factor = head_size ** (-0.5)
    cosine, sine = (cosine_ref[...], sine_ref[...])
    visible = visibility(index_row_ref, index_col_ref, start_ref)
    projected = projected_ref[...].reshape(length, -1)
    mixed_grad = mixed_grad_ref[...].reshape(length, -1)
    gain_query, gain_key = (gain_ref[0:1], gain_ref[1:2])
    key_at = groups * head_size
    key_scale, key_hat, key_rot = head_forward(
        projected[:, key_at : key_at + head_size], gain_key, cosine, sine
    )
    value = projected[:, key_at + head_size :].astype(BF16)
    block = low_ref.shape[:-1] + (head_size,)
    key_grad = jnp.zeros((length, head_size), F32)
    value_grad = jnp.zeros((length, head_size), F32)
    query_gain = jnp.zeros((1, head_size), F32)
    for head in range(groups):
        columns = slice(head * head_size, (head + 1) * head_size)
        query_scale, query_hat, query_rot = head_forward(
            projected[:, columns], gain_query, cosine, sine
        )
        head_grad = mixed_grad[:, columns]
        probs = head_probs(query_rot, key_rot, visible)
        value_grad += matmul(probs.astype(BF16), head_grad, ((0,), (0,)))
        weighted = probs * matmul(head_grad, value, ((1,), (1,)))
        score_grad = (weighted - probs * jnp.sum(weighted, axis=-1, keepdims=True)).astype(BF16)
        key_grad += matmul(score_grad, query_rot, ((0,), (0,)))
        query_grad = factor * matmul(score_grad, key_rot, ((1,), (0,)))
        gain_part, query_low = head_backward(
            query_grad, gain_query, query_scale, query_hat, cosine, sine
        )
        query_gain += gain_part
        low_ref[..., columns] = query_low.reshape(block)
    key_gain, key_low = head_backward(
        factor * key_grad, gain_key, key_scale, key_hat, cosine, sine
    )
    low_ref[..., key_at : key_at + head_size] = key_low.reshape(block)
    low_ref[..., key_at + head_size :] = value_grad.astype(BF16).reshape(block)
    gain_grad_ref[...] = jnp.concatenate(
        [query_gain, key_gain, jnp.zeros((6, head_size), F32)], axis=0
    )


def sequence_specs(blocks, length, columns):
    def token_spec(width):
        return pl.BlockSpec(
            (blocks[0], None, blocks[2], None, blocks[4], width),
            lambda i, j: (0, i, 0, j, 0, 0),
        )

    def table_spec(rows, width):
        return pl.BlockSpec((None, None, rows, width), lambda i, j: (i, j, 0, 0))

    return token_spec, table_spec


def shards(
    tokens,
    segments,
    cotangent,
    w_query,
    key_projection_weight,
    value_projection_weight,
    w_output,
    w_gate,
    w_up,
    w_down,
    gain_attn,
    gain_query,
    gain_key,
    gain_mlp,
):
    outer = lax.axis_size("outer")
    plane = lax.axis_size("inner") * lax.axis_size("seq")
    local_sequences, local_rows, width = tokens.shape
    total_rows = segments.shape[1]
    rows_here = local_sequences * local_rows
    weight_rows = w_query.shape[0]
    head_size = gain_query.shape[0] * outer * plane
    query_columns = w_query.shape[1] // plane
    key_columns = key_projection_weight.shape[1] // plane
    attn_columns = query_columns + 2 * key_columns
    hidden_rows = w_down.shape[0]
    hidden_columns = hidden_rows * outer
    routes = plane_routes(outer)
    seq_index = lax.axis_index("seq")
    first_core = seq_index % 2 == 0

    def by_column(values):
        return values.reshape(values.shape[0], plane, -1).transpose(1, 0, 2)

    def by_hidden(values):
        split = values.reshape(values.shape[0], outer, plane, hidden_rows)
        return split.transpose(2, 0, 1, 3).reshape(plane, values.shape[0], hidden_columns)

    gain_rows = 16
    gain_line = jnp.concatenate([gain_attn, gain_mlp, gain_query, gain_key])
    gain_count = gain_query.shape[0]
    gain_block = jnp.zeros((gain_rows, attn_columns + query_columns), BF16)
    gain_block = gain_block.at[0, : gain_line.shape[0]].set(gain_line)
    attn_send = jnp.concatenate(
        [
            by_column(w_query),
            by_column(key_projection_weight),
            by_column(value_projection_weight),
            by_column(w_output),
        ],
        axis=-1,
    )
    attn_send = jnp.concatenate(
        [attn_send, jnp.broadcast_to(gain_block, (plane,) + gain_block.shape)], axis=1
    )
    attn_part = lax.all_to_all(attn_send, PLANE, 0, 0, tiled=True)
    output_part = attn_part[:, :weight_rows, attn_columns:].reshape(-1, query_columns)
    attn_part = attn_part[:, :, :attn_columns]
    attn_full = lax.all_gather(attn_part, "outer", axis=0)
    w_attn = attn_full[:, :, :weight_rows].reshape(width, attn_columns)
    gain_lines = attn_full[:, :, weight_rows]
    at = 0
    gains = []
    for count in (weight_rows, weight_rows, gain_count, gain_count):
        gains.append(gain_lines[..., at : at + count].reshape(-1).astype(F32))
        at += count
    gain_attn_all, gain_mlp_all, gain_query_all, gain_key_all = gains
    head_gains = jnp.concatenate(
        [gain_query_all[None], gain_key_all[None], jnp.zeros((6, head_size), F32)], axis=0
    )

    output_full = lax.all_gather(output_part, "outer", axis=0, tiled=True)
    w_out = lax.all_to_all(
        output_full.reshape(plane, query_columns, query_columns), PLANE, 0, 0, tiled=True
    )
    w_out = w_out.transpose(1, 0, 2).reshape(query_columns, width)

    mlp_send = jnp.concatenate([by_hidden(w_gate), by_hidden(w_up)], axis=-1)
    mlp_part = lax.all_to_all(mlp_send, PLANE, 0, 0, tiled=True)
    w_mlp = lax.all_gather(
        mlp_part.reshape(plane * weight_rows, 2 * hidden_columns), "outer", axis=0, tiled=True
    )
    w_down_here = lax.all_gather(w_down, "outer", axis=0, tiled=True)

    segments_two = jnp.stack([segments, lax.ppermute(segments, EVERY, routes[3])])
    core, row = (seq_index % 2, seq_index // 2)
    offsets = jnp.stack([(row ^ r) * 2 + (core ^ c) for c in range(2) for r in range(2)])
    token_index = (
        offsets[:, None] * local_rows + jnp.arange(local_rows, dtype=jnp.int32)[None]
    ).reshape(-1)
    segments_here = jnp.take(segments_two, token_index, axis=2)
    doc_start = jnp.sum(
        (segments_two[:, :, None, :] < segments_here[:, :, :, None]).astype(jnp.int32), axis=-1
    )
    positions = (token_index - doc_start).astype(F32)
    half_size = head_size // 2
    frequency = jnp.power(THETA, -(jnp.arange(half_size, dtype=F32) * 2.0 / head_size))
    angles = positions[..., None] * frequency
    cosine, sine = (jnp.cos(angles), jnp.sin(angles))
    cosine = jnp.concatenate([cosine, cosine], axis=-1)
    sine = jnp.concatenate([-sine, sine], axis=-1)
    start_table = doc_start[..., None]
    index_col = token_index[:, None]
    index_row = token_index[None, :]

    blocks = (2, 2, 2, local_sequences, local_rows)
    token_spec, table_spec = sequence_specs(blocks, total_rows, attn_columns)
    table_specs = [
        table_spec(total_rows, head_size),
        table_spec(total_rows, head_size),
        table_spec(total_rows, 1),
        pl.BlockSpec((total_rows, 1), lambda i, j: (0, 0)),
        pl.BlockSpec((1, total_rows), lambda i, j: (0, 0)),
        pl.BlockSpec((8, head_size), lambda i, j: (0, 0)),
    ]
    tables = (cosine, sine, start_table, index_col, index_row, head_gains)
    params = pltpu.CompilerParams(vmem_limit_bytes=VMEM_LIMIT)

    tokens_flat = tokens.reshape(rows_here, width)
    cotangent_flat = cotangent.reshape(rows_here, width)
    tokens_all = plane_gather(tokens_flat, routes, first_core).reshape(-1, width).astype(F32)
    normed = (tokens_all * rms_scale(tokens_all) * gain_attn_all).astype(BF16)
    projected = jnp.dot(normed, w_attn, preferred_element_type=F32)
    projected = projected.reshape(blocks + (attn_columns,))
    mixed = pl.pallas_call(
        attention_kernel,
        grid=(blocks[1], blocks[3]),
        in_specs=[token_spec(attn_columns)] + table_specs,
        out_specs=token_spec(query_columns),
        out_shape=jax.ShapeDtypeStruct(blocks + (query_columns,), BF16),
        compiler_params=params,
        cost_estimate=pl.CostEstimate(
            flops=4 * plane * rows_here * total_rows * query_columns,
            bytes_accessed=plane * rows_here * (4 * attn_columns + 2 * query_columns + 8 * head_size),
            transcendentals=plane * rows_here * total_rows * query_columns // head_size,
        ),
    )(projected, *tables)
    mixed = mixed.reshape(-1, query_columns)
    attn_out = jnp.dot(mixed, w_out, preferred_element_type=F32).astype(BF16)
    tokens_here = tokens_flat.astype(F32)
    middle = tokens_here + plane_scatter(
        attn_out.reshape(plane, rows_here, width), routes, first_core
    )
    scale_two = rms_scale(middle)
    hat_two = middle * scale_two
    normed_two = plane_gather(
        (hat_two * gain_mlp_all).astype(BF16), routes, first_core
    ).reshape(-1, width)
    w_gate_here, w_up_here = (w_mlp[:, :hidden_columns], w_mlp[:, hidden_columns:])
    gate = jnp.dot(normed_two, w_gate_here, preferred_element_type=F32)
    up = jnp.dot(normed_two, w_up_here, preferred_element_type=F32)
    sigma = jax.nn.sigmoid(gate)
    hidden = (gate * sigma * up).astype(BF16)
    down_out = jnp.dot(hidden, w_down_here, preferred_element_type=F32).astype(BF16)
    output = middle + plane_scatter(
        down_out.reshape(plane, rows_here, width), routes, first_core
    )

    cotangent_all = plane_gather(cotangent_flat, routes, first_core).reshape(-1, width)

    def weight_grad(left, right):
        return lax.dot_general(
            left, right, (((0,), (0,)), ((), ())), preferred_element_type=F32
        ).astype(BF16)

    def times_transposed(left, right):
        return lax.dot_general(left, right, (((1,), (1,)), ((), ())), preferred_element_type=F32)

    def sum_planes(values):
        return lax.psum_scatter(values, "outer", scatter_dimension=0, tiled=True)

    down_grad = sum_planes(weight_grad(hidden, cotangent_all))
    hidden_grad = times_transposed(cotangent_all, w_down_here)
    gate_grad = (hidden_grad * up * sigma * (1.0 + gate * (1.0 - sigma))).astype(BF16)
    up_grad = (hidden_grad * gate * sigma).astype(BF16)
    mlp_grad = jnp.concatenate([gate_grad, up_grad], axis=-1)
    mlp_wgrad = sum_planes(weight_grad(normed_two, mlp_grad))
    second_grad = times_transposed(mlp_grad, w_mlp).astype(BF16)
    second_grad = plane_scatter(
        second_grad.reshape(plane, rows_here, width), routes, first_core
    )
    middle_grad = cotangent_flat.astype(F32) + norm_back(
        second_grad * gain_mlp_all, hat_two, scale_two
    )
    out_grad = plane_gather(middle_grad.astype(BF16), routes, first_core).reshape(-1, width)
    mixed_grad = times_transposed(out_grad, w_out).astype(BF16)
    low, gain_parts = pl.pallas_call(
        attention_back_kernel,
        grid=(blocks[1], blocks[3]),
        in_specs=[token_spec(attn_columns), token_spec(query_columns)] + table_specs,
        out_specs=(token_spec(attn_columns), table_spec(8, head_size)),
        out_shape=(
            jax.ShapeDtypeStruct(blocks + (attn_columns,), BF16),
            jax.ShapeDtypeStruct((blocks[1], blocks[3], 8, head_size), F32),
        ),
        compiler_params=params,
        cost_estimate=pl.CostEstimate(
            flops=10 * plane * rows_here * total_rows * query_columns,
            bytes_accessed=plane * rows_here * (6 * attn_columns + 2 * query_columns + 8 * head_size),
            transcendentals=plane * rows_here * total_rows * query_columns // head_size,
        ),
    )(projected, mixed_grad.reshape(blocks + (query_columns,)), *tables)
    low = low.reshape(-1, attn_columns)

    output_wgrad = weight_grad(mixed, out_grad)
    output_wgrad = output_wgrad.reshape(query_columns, plane, query_columns).transpose(1, 0, 2)
    output_wgrad = lax.all_to_all(output_wgrad, PLANE, 0, 0, tiled=True)
    output_wgrad = sum_planes(output_wgrad.reshape(width, query_columns))

    head_gain_grad = jnp.sum(gain_parts, axis=(0, 1))[:2].reshape(-1)
    gain_lines = jnp.zeros((outer, gain_rows, attn_columns), BF16)
    gain_lines = gain_lines.at[:, 0, : 2 * head_size].set(
        jnp.broadcast_to(head_gain_grad.astype(BF16), (outer, 2 * head_size))
    )
    attn_wgrad = jnp.concatenate(
        [weight_grad(normed, low).reshape(outer, -1, attn_columns), gain_lines], axis=1
    )
    attn_wgrad = sum_planes(attn_wgrad.reshape(-1, attn_columns))

    normed_grad = times_transposed(low, w_attn).astype(BF16)
    normed_grad = plane_scatter(
        normed_grad.reshape(plane, rows_here, width), routes, first_core
    )
    scale_one = rms_scale(tokens_here)
    input_grad = middle_grad + norm_back(
        normed_grad * gain_attn_all, tokens_here * scale_one, scale_one
    )

    mlp_back = lax.all_to_all(
        mlp_wgrad.reshape(plane, weight_rows, 2 * hidden_columns), PLANE, 0, 0, tiled=True
    )

    def hidden_back(values):
        split = values.reshape(plane, weight_rows, outer, hidden_rows).transpose(1, 2, 0, 3)
        return split.reshape(weight_rows, -1).astype(F32)

    gate_sum = hidden_back(mlp_back[..., :hidden_columns])
    up_sum = hidden_back(mlp_back[..., hidden_columns:])

    attn_rows = attn_wgrad[: plane * weight_rows].reshape(plane, weight_rows, attn_columns)
    gain_send = jnp.broadcast_to(
        attn_wgrad[plane * weight_rows :], (plane, gain_rows, attn_columns)
    )
    attn_send = jnp.concatenate([attn_rows, gain_send], axis=1)
    attn_back = lax.all_to_all(attn_send, PLANE, 0, 0, tiled=True)
    output_back = lax.all_to_all(
        output_wgrad.reshape(plane, weight_rows, query_columns), PLANE, 0, 0, tiled=True
    )

    def column_back(values):
        return values.transpose(1, 0, 2).reshape(weight_rows, -1).astype(F32)

    attn_rows = attn_back[:, :weight_rows]
    query_sum = column_back(attn_rows[..., :query_columns])
    key_sum = column_back(attn_rows[..., query_columns : query_columns + key_columns])
    value_sum = column_back(attn_rows[..., query_columns + key_columns :])
    output_sum = column_back(output_back)
    head_gain_sum = jnp.sum(attn_back[:, weight_rows, : 2 * head_size].astype(F32), axis=0)
    place = lax.axis_index(EVERY) * gain_count
    query_gain_sum = lax.dynamic_slice_in_dim(head_gain_sum, place, gain_count)
    key_gain_sum = lax.dynamic_slice_in_dim(head_gain_sum, head_size + place, gain_count)

    def gain_sum(gain, *pairs):
        total = sum(jnp.sum(weight.astype(F32) * grad, axis=-1) for weight, grad in pairs)
        return total / gain.astype(F32)

    mlp_gain_sum = gain_sum(gain_mlp, (w_gate, gate_sum), (w_up, up_sum))
    attn_gain_sum = gain_sum(
        gain_attn,
        (w_query, query_sum),
        (key_projection_weight, key_sum),
        (value_projection_weight, value_sum),
    )
    return (
        output.astype(BF16).reshape(tokens.shape),
        input_grad.astype(BF16).reshape(tokens.shape),
        query_sum,
        key_sum,
        value_sum,
        output_sum,
        gate_sum,
        up_sum,
        down_grad.astype(F32),
        attn_gain_sum,
        query_gain_sum,
        key_gain_sum,
        mlp_gain_sum,
    )


def solution(mesh):
    seq = mesh.shape["seq"]
    split = Mesh(mesh.devices.reshape(-1, 2, seq), EVERY)
    rows = P(("outer", "inner"), "seq", None)
    weight = P(EVERY, None)
    gain = P(EVERY)
    return jax.shard_map(
        shards,
        mesh=split,
        in_specs=(rows, P(("outer", "inner"), None), rows) + (weight,) * 7 + (gain,) * 4,
        out_specs=(rows, rows) + (weight,) * 7 + (gain,) * 4,
        check_vma=False,
    )
```

```python
import functools

import jax
import jax.numpy as jnp
from jax import lax
from jax.experimental import pallas as pl
from jax.experimental.pallas import tpu as pltpu
from jax.sharding import Mesh
from jax.sharding import PartitionSpec as P

EPSILON = 1e-06
THETA = 1000000.0
PLANE = ("inner", "seq")
EVERY = ("outer", "inner", "seq")
BF16 = jnp.bfloat16
F32 = jnp.float32
VMEM_LIMIT = 56 * 1024 * 1024
MLP_VMEM_LIMIT = 40 * 1024 * 1024
CHEAP = pl.CostEstimate(flops=1, bytes_accessed=1, transcendentals=0)


def rms_scale(values):
    return lax.rsqrt(jnp.mean(values * values, axis=-1, keepdims=True) + EPSILON)


def norm_back(normalized_grad, normalized, inverse_rms):
    return inverse_rms * (
        normalized_grad
        - normalized * jnp.mean(normalized_grad * normalized, axis=-1, keepdims=True)
    )


def after(value, *others):
    return lax.optimization_barrier((value,) + others)[0]


def plane_routes(outer):
    def pairs(flip):
        out = []
        for o in range(outer):
            for x in range(2):
                for y in range(2):
                    for c in range(2):
                        fx, fy, fc = flip(c)
                        source = ((o * 2 + x) * 2 + y) * 2 + c
                        target = ((o * 2 + (x ^ fx)) * 2 + (y ^ fy)) * 2 + (c ^ fc)
                        out.append((source, target))
        return out

    return (
        pairs(lambda c: (1, 0, 0) if c == 0 else (0, 1, 0)),
        pairs(lambda c: (0, 1, 0) if c == 0 else (1, 0, 0)),
        pairs(lambda c: (0, 0, 1)),
        pairs(lambda c: (1, 0, 0)),
    )


def plane_gather(block, routes, first_core):
    route_a, route_b, route_c, _ = routes
    near_a = lax.ppermute(block, EVERY, route_a)
    near_b = lax.ppermute(block, EVERY, route_b)
    far = lax.ppermute(near_a, EVERY, route_b)
    here = [
        block,
        jnp.where(first_core, near_b, near_a),
        jnp.where(first_core, near_a, near_b),
        far,
    ]
    blocks = [part for block in here for part in (block, lax.ppermute(block, EVERY, route_c))]
    return blocks, (near_a, near_b)


def plane_scatter(blocks, routes, first_core, *needed):
    route_a, route_b, route_c, _ = routes
    other = [lax.ppermute(blocks[at], EVERY, route_c).astype(F32) for at in (7, 5, 3, 1)]
    far = (blocks[6].astype(F32) + other[0]).astype(BF16)
    far = lax.ppermute(far, EVERY, route_b)
    near_x = blocks[4].astype(F32) + other[1]
    near_y = blocks[2].astype(F32) + other[2]
    near_a = jnp.where(first_core, near_x, near_y)
    near_b = jnp.where(first_core, near_y, near_x).astype(BF16)
    from_b = lax.ppermute(near_b, EVERY, route_b)
    near_a = (near_a + far.astype(F32)).astype(BF16)
    if needed:
        near_a = after(near_a, *needed)
    from_a = lax.ppermute(near_a, EVERY, route_a)
    total = blocks[0].astype(F32) + other[3] + from_b.astype(F32) + from_a.astype(F32)
    return total, (far, from_b), from_a


def head_routes(outer, plane, spread):
    routes = []
    for shift in range(outer):
        pairs = []
        for o in range(outer):
            for g in range(plane):
                target = (g + shift) % outer * (plane // spread) + g // spread
                pairs.append((o * plane + g, o * plane + target))
        routes.append(pairs)
    return routes


def heads_gather(rows, head_rows):
    outer, here, width = rows.shape
    plane = lax.axis_size(PLANE)
    me = lax.axis_index(PLANE)
    if plane * head_rows != outer * plane * here or plane * here != head_rows * (plane // outer):
        full = lax.all_gather(rows, PLANE, axis=1, tiled=True).reshape(-1, width)
        return lax.dynamic_slice_in_dim(full, me * head_rows, head_rows)
    arrived = jnp.stack(
        [
            lax.ppermute(
                lax.dynamic_index_in_dim(rows, (me + shift) % outer, 0, False), EVERY, route
            )
            for shift, route in enumerate(head_routes(outer, plane, outer))
        ]
    )
    slab = me // (plane // outer)
    return jnp.concatenate(
        [
            lax.dynamic_index_in_dim(arrived, (slab - place) % outer, 0, False)
            for place in range(outer)
        ]
    )


def heads_scatter(grad, outer):
    head_rows, width = grad.shape
    plane = lax.axis_size(PLANE)
    me = lax.axis_index(PLANE)
    here = head_rows // outer
    if plane * here != head_rows * (plane // outer):
        full = lax.all_gather(grad, PLANE, axis=0, tiled=True)
        full = full.reshape(outer, plane, here, width)
        return lax.dynamic_index_in_dim(full, me, 1, False)
    blocks = grad.reshape(outer, here, width)
    slab = me // (plane // outer)
    arrived = jnp.stack(
        [
            lax.ppermute(
                lax.dynamic_index_in_dim(blocks, (slab - shift) % outer, 0, False),
                EVERY,
                [(target, source) for source, target in route],
            )
            for shift, route in enumerate(head_routes(outer, plane, outer))
        ]
    )
    return jnp.stack(
        [
            lax.dynamic_index_in_dim(arrived, (place - me) % outer, 0, False)
            for place in range(outer)
        ]
    )


def turn(values):
    return pltpu.roll(values, values.shape[-1] // 2, 1)


def head_forward(projected, gain, cosine, sine):
    scale = rms_scale(projected)
    hat = projected * scale
    scaled = hat * gain
    return scale, hat, (scaled * cosine + turn(scaled) * sine).astype(BF16)


def head_backward(rotated_grad, gain, scale, hat, cosine, sine):
    grad = rotated_grad * cosine - turn(rotated_grad) * sine
    gain_grad = jnp.sum(grad * hat, axis=0, keepdims=True)
    return gain_grad, norm_back(grad * gain, hat, scale).astype(BF16)


def matmul(left, right, dims):
    return lax.dot_general(left, right, (dims, ((), ())), preferred_element_type=F32)


def head_probs(query_rot, key_rot, visible):
    head_size = query_rot.shape[-1]
    raw = matmul(query_rot, key_rot, ((1,), (1,))) * head_size ** (-0.5)
    masked = jnp.where(visible, raw, -1e30)
    exponent = jnp.exp(masked - jnp.max(masked, axis=-1, keepdims=True))
    return exponent / jnp.sum(exponent, axis=-1, keepdims=True)


def visibility(index_row_ref, index_col_ref, start_ref):
    index_row = index_row_ref[...]
    return (index_row >= start_ref[...]) & (index_row <= index_col_ref[...])


def attention_kernel(
    block_0,
    block_1,
    block_2,
    block_3,
    gain_attn_ref,
    w_attn_ref,
    w_out_ref,
    cosine_ref,
    sine_ref,
    start_ref,
    index_col_ref,
    index_row_ref,
    gain_ref,
    *refs,
):
    normed_ref, projected_ref, mixed_ref = refs[-8:-5]
    out_refs = refs[-5:-1]
    weight_ref = refs[-1]
    head_size = cosine_ref.shape[-1]
    length = cosine_ref.shape[0]
    groups = mixed_ref.shape[-1] // head_size
    cosine, sine = (cosine_ref[...], sine_ref[...])
    gain_attn = gain_attn_ref[...]
    parts = w_attn_ref.shape[0]
    rows = weight_ref.shape[0] // parts

    @pl.when(pl.program_id(0) == 0)
    def _():
        for at in range(parts):
            weight_ref[at * rows : (at + 1) * rows] = w_attn_ref[at, :rows]

    for at, block_ref in enumerate((block_0, block_1, block_2, block_3)):
        rows = block_ref[...].astype(F32)
        normed_ref[at // 2, at % 2] = (rows * rms_scale(rows) * gain_attn).astype(BF16)
    normed = normed_ref[...].reshape(length, -1)
    projected = matmul(normed, weight_ref[...], ((1,), (0,)))
    projected_ref[...] = projected.reshape(projected_ref.shape)
    visible = visibility(index_row_ref, index_col_ref, start_ref)
    gain_query, gain_key = (gain_ref[0:1], gain_ref[1:2])
    key_at = groups * head_size
    _, _, key_rot = head_forward(
        projected[:, key_at : key_at + head_size], gain_key, cosine, sine
    )
    value = projected[:, key_at + head_size :].astype(BF16)
    heads = []
    for head in range(groups):
        columns = slice(head * head_size, (head + 1) * head_size)
        _, _, query_rot = head_forward(projected[:, columns], gain_query, cosine, sine)
        probs = head_probs(query_rot, key_rot, visible).astype(BF16)
        heads.append(matmul(probs, value, ((1,), (0,))).astype(BF16))
    mixed = jnp.concatenate(heads, axis=1)
    mixed_ref[...] = mixed.reshape(mixed_ref.shape)
    out = matmul(mixed, w_out_ref[...], ((1,), (0,))).astype(BF16)
    rows = length // len(out_refs)
    for at, out_ref in enumerate(out_refs):
        out_ref[...] = out[at * rows : (at + 1) * rows]


def attention_back_kernel(
    block_0,
    block_1,
    block_2,
    block_3,
    projected_ref,
    w_out_ref,
    cosine_ref,
    sine_ref,
    start_ref,
    index_col_ref,
    index_row_ref,
    gain_ref,
    *refs,
):
    low_ref, gain_grad_ref = refs[-2:]
    head_size = cosine_ref.shape[-1]
    length = cosine_ref.shape[0]
    groups = w_out_ref.shape[0] // head_size
    factor = head_size ** (-0.5)
    cosine, sine = (cosine_ref[...], sine_ref[...])
    visible = visibility(index_row_ref, index_col_ref, start_ref)
    projected = projected_ref[...].reshape(length, -1)
    out_grad = jnp.concatenate(
        [block_0[...], block_1[...], block_2[...], block_3[...]], axis=0
    )
    mixed_grad = matmul(out_grad, w_out_ref[...], ((1,), (1,))).astype(BF16)
    gain_query, gain_key = (gain_ref[0:1], gain_ref[1:2])
    key_at = groups * head_size
    key_scale, key_hat, key_rot = head_forward(
        projected[:, key_at : key_at + head_size], gain_key, cosine, sine
    )
    value = projected[:, key_at + head_size :].astype(BF16)
    block = low_ref.shape[:-1] + (head_size,)
    key_grad = jnp.zeros((length, head_size), F32)
    value_grad = jnp.zeros((length, head_size), F32)
    query_gain = jnp.zeros((1, head_size), F32)
    for head in range(groups):
        columns = slice(head * head_size, (head + 1) * head_size)
        query_scale, query_hat, query_rot = head_forward(
            projected[:, columns], gain_query, cosine, sine
        )
        head_grad = mixed_grad[:, columns]
        probs = head_probs(query_rot, key_rot, visible)
        value_grad += matmul(probs.astype(BF16), head_grad, ((0,), (0,)))
        weighted = probs * matmul(head_grad, value, ((1,), (1,)))
        score_grad = (weighted - probs * jnp.sum(weighted, axis=-1, keepdims=True)).astype(BF16)
        key_grad += matmul(score_grad, query_rot, ((0,), (0,)))
        query_grad = factor * matmul(score_grad, key_rot, ((1,), (0,)))
        gain_part, query_low = head_backward(
            query_grad, gain_query, query_scale, query_hat, cosine, sine
        )
        query_gain += gain_part
        low_ref[..., columns] = query_low.reshape(block)
    key_gain, key_low = head_backward(
        factor * key_grad, gain_key, key_scale, key_hat, cosine, sine
    )
    low_ref[..., key_at : key_at + head_size] = key_low.reshape(block)
    low_ref[..., key_at + head_size :] = value_grad.astype(BF16).reshape(block)
    gain_grad_ref[...] = jnp.concatenate(
        [query_gain, key_gain, jnp.zeros((6, head_size), F32)], axis=0
    )


def mlp_forward_kernel(*refs, count):
    chunk_refs = refs[:count]
    w_mlp_ref = refs[count]
    gate_ref, up_ref, hidden_ref, held_ref = refs[-4:]
    pair = pl.program_id(1)
    rows = chunk_refs[0].shape[0]

    def hold(at):
        held_ref[at, :rows] = chunk_refs[2 * at][...]
        held_ref[at, rows:] = chunk_refs[2 * at + 1][...]

    for at in range(count // 2):
        pl.when((pl.program_id(0) == 0) & (pair == at))(functools.partial(hold, at))
    chunk = held_ref[pair]
    step = gate_ref.shape[-1]
    at = pl.multiple_of(pl.program_id(0) * step, step)
    half = w_mlp_ref.shape[1] // 2
    gate = matmul(chunk, w_mlp_ref[:, pl.ds(at, step)], ((1,), (0,)))
    up = matmul(chunk, w_mlp_ref[:, pl.ds(half + at, step)], ((1,), (0,)))
    gate_ref[...] = gate.reshape(gate_ref.shape)
    up_ref[...] = up.reshape(gate_ref.shape)
    hidden_ref[...] = (gate * jax.nn.sigmoid(gate) * up).astype(BF16).reshape(gate_ref.shape)


def mlp_forward(base, chunks, w_mlp, params, *kept):
    count = len(chunks)
    rows, width = chunks[0].shape
    columns = w_mlp.shape[1] // 2
    step = 256 if columns % 256 == 0 else columns
    tiles = columns // step
    shape = (8, rows, columns)
    out_spec = pl.BlockSpec((2, rows, step), lambda j, i: (base + i, 0, j))
    return pl.pallas_call(
        functools.partial(mlp_forward_kernel, count=count),
        grid=(tiles, count // 2),
        in_specs=[pl.BlockSpec((rows, width), lambda j, i: (0, 0))] * count
        + [pl.BlockSpec(memory_space=pltpu.VMEM)]
        + [pl.BlockSpec(memory_space=pl.ANY)] * len(kept),
        out_specs=(out_spec,) * 3,
        out_shape=(
            jax.ShapeDtypeStruct(shape, F32),
            jax.ShapeDtypeStruct(shape, F32),
            jax.ShapeDtypeStruct(shape, BF16),
        ),
        scratch_shapes=[pltpu.VMEM((count // 2, 2 * rows, width), BF16)],
        input_output_aliases={count + 1 + at: at for at in range(len(kept))},
        compiler_params=params,
        cost_estimate=CHEAP,
    )(*chunks, w_mlp, *kept)


def mlp_backward_kernel(
    cotangent_ref, gate_ref, up_ref, w_down_ref, w_mlp_ref, *refs, count
):
    grad_ref = refs[-count - 1]
    second_refs = refs[-count:]
    pair, rows, columns = gate_ref.shape
    cotangent = cotangent_ref[...].reshape(pair * rows, -1)
    hidden_grad = matmul(cotangent, w_down_ref[...], ((1,), (1,)))
    gate = gate_ref[...].reshape(pair * rows, -1)
    up = up_ref[...].reshape(pair * rows, -1)
    sigma = jax.nn.sigmoid(gate)
    gate_grad = hidden_grad * up * sigma * (1.0 + gate * (1.0 - sigma))
    up_grad = hidden_grad * gate * sigma
    grad = jnp.concatenate([gate_grad.astype(BF16), up_grad.astype(BF16)], axis=1)
    grad_ref[...] = grad.reshape(grad_ref.shape)
    second = matmul(grad, w_mlp_ref[...], ((1,), (1,))).astype(BF16)

    def store(at):
        second_refs[at][...] = second[:rows]
        second_refs[at + 1][...] = second[rows:]

    for at in range(0, count, 2):
        pl.when(pl.program_id(0) == at // 2)(functools.partial(store, at))


def mlp_backward(base, count, operands, params, *kept):
    cotangent, gate, _, w_down, w_mlp = operands
    _, rows, width = cotangent.shape
    columns = gate.shape[-1]

    def pair_spec(last):
        return pl.BlockSpec((2, rows, last), lambda i: (base + i, 0, 0))

    return pl.pallas_call(
        functools.partial(mlp_backward_kernel, count=count),
        grid=(count // 2,),
        in_specs=[
            pair_spec(width),
            pair_spec(columns),
            pair_spec(columns),
            pl.BlockSpec(memory_space=pltpu.VMEM),
            pl.BlockSpec(memory_space=pltpu.VMEM),
        ]
        + [pl.BlockSpec(memory_space=pl.ANY)] * len(kept),
        out_specs=(pair_spec(2 * columns),)
        + (pl.BlockSpec((rows, width), lambda i: (0, 0)),) * count,
        out_shape=(jax.ShapeDtypeStruct((8, rows, 2 * columns), BF16),)
        + (jax.ShapeDtypeStruct((rows, width), BF16),) * count,
        input_output_aliases={5 + at: at for at in range(len(kept))},
        compiler_params=params,
        cost_estimate=pl.CostEstimate(
            flops=6 * count * rows * width * columns, bytes_accessed=10**7, transcendentals=0
        ),
    )(*operands, *kept)


def pack_kernel(gate_ref, up_ref, out_ref, *, step):
    plane, _, columns = out_ref.shape
    hidden = columns // 2
    for g in range(plane):
        for at, ref in enumerate((gate_ref, up_ref)):
            parts = [
                ref[:, start + g * step : start + (g + 1) * step]
                for start in range(0, ref.shape[1], plane * step)
            ]
            out_ref[g, :, at * hidden : (at + 1) * hidden] = jnp.concatenate(parts, axis=1)


def unpack_kernel(back_ref, gate_ref, up_ref, gain_ref, gate_out, up_out, gain_out, *, step):
    plane, _, columns = back_ref.shape
    hidden = columns // 2
    total = 0.0
    for at, (weight_ref, out_ref) in enumerate(((gate_ref, gate_out), (up_ref, up_out))):
        parts = [
            back_ref[g, :, at * hidden + start : at * hidden + start + step]
            for start in range(0, hidden, step)
            for g in range(plane)
        ]
        grad = jnp.concatenate(parts, axis=1).astype(F32)
        out_ref[...] = grad
        total += jnp.sum(grad * weight_ref[...].astype(F32), axis=1, keepdims=True)
    gain_out[...] = total / gain_ref[...]


def shards(
    tokens,
    segments,
    cotangent,
    w_query,
    key_projection_weight,
    value_projection_weight,
    w_output,
    w_gate,
    w_up,
    w_down,
    gain_attn,
    gain_query,
    gain_key,
    gain_mlp,
):
    outer = lax.axis_size("outer")
    plane = lax.axis_size("inner") * lax.axis_size("seq")
    local_sequences, local_rows, width = tokens.shape
    total_rows = segments.shape[1]
    rows_here = local_sequences * local_rows
    weight_rows = w_query.shape[0]
    head_size = gain_query.shape[0] * outer * plane
    query_columns = w_query.shape[1] // plane
    key_columns = key_projection_weight.shape[1] // plane
    attn_columns = query_columns + 2 * key_columns
    hidden_rows = w_down.shape[0]
    hidden_columns = hidden_rows * outer
    routes = plane_routes(outer)
    seq_index = lax.axis_index("seq")
    first_core = seq_index % 2 == 0

    tokens_flat = tokens.reshape(rows_here, width)
    segments_there = lax.ppermute(segments, EVERY, routes[3])
    tokens_all, tokens_near = plane_gather(tokens_flat, routes, first_core)

    def by_column(values):
        return values.reshape(values.shape[0], plane, -1).transpose(1, 0, 2)

    gain_rows = 8
    gain_count = gain_query.shape[0]
    gain_line = jnp.concatenate([gain_attn, gain_mlp, gain_query, gain_key])
    gain_line = jnp.pad(
        gain_line[None], ((0, gain_rows - 1), (0, attn_columns - gain_line.shape[0]))
    )
    output_rows = lax.all_gather(w_output, "outer", axis=0)
    attn_send = jnp.concatenate(
        [by_column(w_query), by_column(key_projection_weight), by_column(value_projection_weight)],
        axis=-1,
    )
    attn_send = jnp.concatenate(
        [attn_send, jnp.broadcast_to(gain_line, (plane,) + gain_line.shape)], axis=1
    )
    attn_part = lax.all_to_all(
        after(attn_send, segments_there, *tokens_near), PLANE, 0, 0, tiled=True)
    attn_full = lax.all_gather(after(attn_part, output_rows), "outer", axis=0, tiled=True)
    w_attn = attn_full[:, :weight_rows].reshape(width, attn_columns)
    gain_lines = attn_full[:, weight_rows]
    at = 0
    gains = []
    for count in (weight_rows, weight_rows, gain_count, gain_count):
        gains.append(gain_lines[:, at : at + count].reshape(-1).astype(F32))
        at += count
    gain_attn_all, gain_mlp_all, gain_query_all, gain_key_all = gains
    head_gains = jnp.concatenate(
        [gain_query_all[None], gain_key_all[None], jnp.zeros((6, head_size), F32)], axis=0
    )

    params = pltpu.CompilerParams(vmem_limit_bytes=VMEM_LIMIT)
    mlp_send = pl.pallas_call(
        functools.partial(pack_kernel, step=hidden_rows),
        out_shape=jax.ShapeDtypeStruct((plane, weight_rows, 2 * hidden_columns), BF16),
        compiler_params=params,
        cost_estimate=CHEAP,
    )(w_gate, w_up)
    mlp_part = lax.all_to_all(
        after(mlp_send, attn_part), PLANE, 0, 0, tiled=True
    )
    w_mlp = lax.all_gather(
        mlp_part.reshape(plane * weight_rows, 2 * hidden_columns), "outer", axis=0, tiled=True
    )

    segments_two = jnp.stack([segments, segments_there])
    core, row = (seq_index % 2, seq_index // 2)
    offsets = jnp.stack([(row ^ r) * 2 + (core ^ c) for r in range(2) for c in range(2)])
    token_index = (
        offsets[:, None] * local_rows + jnp.arange(local_rows, dtype=jnp.int32)[None]
    ).reshape(-1)
    segments_here = jnp.take(segments_two, token_index, axis=2)
    doc_start = jnp.sum(
        (segments_two[:, :, None, :] < segments_here[:, :, :, None]).astype(jnp.int32), axis=-1
    )
    positions = (token_index - doc_start).astype(F32)
    half_size = head_size // 2
    frequency = jnp.power(THETA, -(jnp.arange(half_size, dtype=F32) * 2.0 / head_size))
    angles = positions[..., None] * frequency
    cosine, sine = (jnp.cos(angles), jnp.sin(angles))
    cosine = jnp.concatenate([cosine, cosine], axis=-1)
    sine = jnp.concatenate([-sine, sine], axis=-1)
    start_table = doc_start[..., None]
    index_col = token_index[:, None]
    index_row = token_index[None, :]
    w_out = heads_gather(after(output_rows, mlp_part, cosine, sine, start_table), query_columns)

    blocks = (2, 2, 2, local_sequences, local_rows)
    tables = (cosine, sine, start_table, index_col, index_row, head_gains)
    def whole_spec(value):
        return pl.BlockSpec(value.shape, lambda *at: (0,) * value.ndim)

    def specs_of(side):
        def token_spec(columns):
            return pl.BlockSpec(
                (None, 2, 2, None, local_rows, columns),
                lambda *at: (side, 0, 0, at[-1], 0, 0),
            )

        def table_spec(rows, columns):
            return pl.BlockSpec(
                (None, None, rows, columns), lambda *at: (side, at[-1], 0, 0)
            )

        return (
            token_spec,
            table_spec,
            [
                table_spec(total_rows, head_size),
                table_spec(total_rows, head_size),
                table_spec(total_rows, 1),
                whole_spec(index_col),
                whole_spec(index_row),
                whole_spec(head_gains),
            ],
        )

    chunk_spec = pl.BlockSpec((local_rows, width), lambda *at: (at[-1], 0))

    def attention_forward(side, chunks, *kept):
        token_spec, _, table_specs = specs_of(side)
        operands = (*chunks, gain_attn_all[None], attn_full, w_out) + tables
        return pl.pallas_call(
            attention_kernel,
            grid=(local_sequences,),
            in_specs=[chunk_spec] * 4
            + [
                pl.BlockSpec((1, width), lambda *at: (0, 0)),
                whole_spec(attn_full),
                whole_spec(w_out),
            ]
            + table_specs
            + [pl.BlockSpec(memory_space=pl.ANY)] * len(kept),
            out_specs=(
                token_spec(width),
                token_spec(attn_columns),
                token_spec(query_columns),
            )
            + (chunk_spec,) * 4,
            out_shape=(
                jax.ShapeDtypeStruct(blocks + (width,), BF16),
                jax.ShapeDtypeStruct(blocks + (attn_columns,), F32),
                jax.ShapeDtypeStruct(blocks + (query_columns,), BF16),
            )
            + (jax.ShapeDtypeStruct((rows_here, width), BF16),) * 4,
            scratch_shapes=[pltpu.VMEM((width, attn_columns), BF16)],
            input_output_aliases={len(operands) + at: at for at in range(len(kept))},
            compiler_params=params,
            cost_estimate=CHEAP,
        )(*operands, *kept)

    def attention_backward(side, chunks, *kept):
        token_spec, table_spec, table_specs = specs_of(side)
        operands = (*chunks, projected, w_out) + tables
        return pl.pallas_call(
            attention_back_kernel,
            grid=(local_sequences,),
            in_specs=[chunk_spec] * 4
            + [token_spec(attn_columns), whole_spec(w_out)]
            + table_specs
            + [pl.BlockSpec(memory_space=pl.ANY)] * len(kept),
            out_specs=(
                token_spec(attn_columns),
                pl.BlockSpec((None, 8, head_size), lambda *at: (at[-1], 0, 0)),
            ),
            out_shape=(
                jax.ShapeDtypeStruct(blocks + (attn_columns,), BF16),
                jax.ShapeDtypeStruct((local_sequences, 8, head_size), F32),
            ),
            input_output_aliases={len(operands) + at: at for at in range(len(kept))},
            compiler_params=params,
            cost_estimate=CHEAP,
        )(*operands, *kept)

    cotangent_flat = cotangent.reshape(rows_here, width)
    cotangent_all, cotangent_near = plane_gather(
        after(cotangent_flat, w_out, mlp_part, *tokens_all), routes, first_core
    )
    cotangent_all = jnp.stack(cotangent_all)
    tokens_all = after(tuple(tokens_all), mlp_part)
    *kept, there_0, there_1, there_2, there_3 = attention_forward(1, tokens_all[4:])
    *kept, here_0, here_1, here_2, here_3 = attention_forward(
        0, after(tokens_all, *cotangent_near)[:4], *kept
    )
    normed, projected, mixed = kept
    normed = normed.reshape(-1, width)
    mixed = mixed.reshape(-1, query_columns)
    w_down_here = lax.all_gather(after(w_down, mixed), "outer", axis=0, tiled=True)
    tokens_here = tokens_flat.astype(F32)
    attn_out = [here_0, here_1, here_2, here_3, there_0, there_1, there_2, there_3]
    middle = tokens_here + plane_scatter(attn_out, routes, first_core)[0]
    scale_two = rms_scale(middle)
    hat_two = middle * scale_two
    normed_two, _ = plane_gather(
        (hat_two * gain_mlp_all).astype(BF16), routes, first_core
    )
    mlp_params = pltpu.CompilerParams(vmem_limit_bytes=MLP_VMEM_LIMIT)
    kept = mlp_forward(0, normed_two[:6], w_mlp, mlp_params)
    gate, up, hidden = mlp_forward(3, normed_two[6:], w_mlp, mlp_params, *kept)
    normed_two = jnp.stack(normed_two).reshape(-1, width)
    hidden = hidden.reshape(-1, hidden_columns)
    def weight_grad(left, right):
        return lax.dot_general(
            left, right, (((0,), (0,)), ((), ())), preferred_element_type=F32
        ).astype(BF16)

    def times_transposed(left, right):
        return lax.dot_general(left, right, (((1,), (1,)), ((), ())), preferred_element_type=F32)

    def sum_planes(values):
        return lax.psum_scatter(values, "outer", scatter_dimension=0, tiled=True)

    cotangent_flat_all = cotangent_all.reshape(-1, width)
    down_grad = weight_grad(hidden, cotangent_flat_all)
    down_sum = sum_planes(down_grad)
    operands = (after(cotangent_all, down_grad), gate, up, w_down_here, w_mlp)
    mlp_grad, *far = mlp_backward(3, 2, operands, mlp_params)
    mlp_grad, *near = mlp_backward(1, 4, operands, mlp_params, mlp_grad)
    mlp_grad, *own = mlp_backward(0, 2, operands, mlp_params, mlp_grad)
    second = own + near + far
    mlp_grad = mlp_grad.reshape(-1, 2 * hidden_columns)
    mlp_part_grad = weight_grad(normed_two, mlp_grad)
    mlp_wgrad = sum_planes(after(mlp_part_grad, down_sum))
    down_out = jnp.dot(
        after(hidden, *own), w_down_here, preferred_element_type=F32
    ).astype(BF16)
    second_grad = plane_scatter(
        second, routes, first_core, down_sum
    )[0]
    middle_grad = cotangent_flat.astype(F32) + norm_back(
        after(second_grad, mlp_part_grad) * gain_mlp_all, hat_two, scale_two
    )
    out_blocks, _ = plane_gather(middle_grad.astype(BF16), routes, first_core)
    out_grad = jnp.stack(out_blocks).reshape(-1, width)
    output, output_far, output_near = plane_scatter(
        after(down_out, out_grad).reshape(plane, rows_here, width), routes, first_core
    )
    output = middle + output
    low, gain_here = attention_backward(0, out_blocks[:4])
    low, gain_there = attention_backward(1, out_blocks[4:], low)
    low = after(low.reshape(-1, attn_columns), mlp_wgrad, *output_far)

    head_gain_grad = jnp.sum(gain_here + gain_there, axis=0)[:2].reshape(-1)
    gain_lines = jnp.zeros((outer, gain_rows, attn_columns), BF16)
    gain_lines = gain_lines.at[:, 0, : 2 * head_size].set(
        jnp.broadcast_to(head_gain_grad.astype(BF16), (outer, 2 * head_size))
    )
    attn_wgrad = jnp.concatenate(
        [weight_grad(normed, low).reshape(outer, -1, attn_columns), gain_lines], axis=1
    )
    attn_part = attn_wgrad
    attn_wgrad = sum_planes(after(attn_wgrad.reshape(-1, attn_columns), mlp_wgrad))
    output_wgrad = weight_grad(after(mixed, attn_part), out_grad)
    normed_grad = times_transposed(after(low, output_wgrad), w_attn).astype(BF16)
    output_wgrad = heads_scatter(output_wgrad, outer).reshape(-1, width)
    output_wgrad = sum_planes(after(output_wgrad, attn_wgrad))
    normed_grad = plane_scatter(
        after(normed_grad, output_near).reshape(plane, rows_here, width), routes, first_core
    )[0]
    mlp_back = lax.all_to_all(
        mlp_wgrad.reshape(plane, weight_rows, 2 * hidden_columns), PLANE, 0, 0, tiled=True
    )

    gate_sum, up_sum, mlp_gain_sum = pl.pallas_call(
        functools.partial(unpack_kernel, step=hidden_rows),
        out_shape=(
            jax.ShapeDtypeStruct(w_gate.shape, F32),
            jax.ShapeDtypeStruct(w_up.shape, F32),
            jax.ShapeDtypeStruct((weight_rows, 1), F32),
        ),
        compiler_params=params,
        cost_estimate=CHEAP,
    )(mlp_back, w_gate, w_up, gain_mlp.astype(F32)[:, None])

    attn_rows = attn_wgrad[: plane * weight_rows].reshape(plane, weight_rows, attn_columns)
    gain_send = jnp.broadcast_to(
        attn_wgrad[plane * weight_rows :], (plane, gain_rows, attn_columns)
    )
    attn_send = jnp.concatenate([attn_rows, gain_send], axis=1)
    attn_back = lax.all_to_all(attn_send, PLANE, 0, 0, tiled=True)
    scale_one = rms_scale(tokens_here)
    input_grad = middle_grad + norm_back(
        after(normed_grad, attn_back) * gain_attn_all, tokens_here * scale_one, scale_one
    )

    attn_back = after(attn_back, output_wgrad)
    def column_back(values):
        return values.transpose(1, 0, 2).reshape(weight_rows, -1).astype(F32)

    attn_rows = attn_back[:, :weight_rows]
    query_sum = column_back(attn_rows[..., :query_columns])
    key_sum = column_back(attn_rows[..., query_columns : query_columns + key_columns])
    value_sum = column_back(attn_rows[..., query_columns + key_columns :])
    output_sum = output_wgrad.astype(F32)
    head_gain_sum = jnp.sum(attn_back[:, weight_rows, : 2 * head_size].astype(F32), axis=0)
    place = lax.axis_index(EVERY) * gain_count
    query_gain_sum = lax.dynamic_slice_in_dim(head_gain_sum, place, gain_count)
    key_gain_sum = lax.dynamic_slice_in_dim(head_gain_sum, head_size + place, gain_count)

    def gain_sum(gain, *pairs):
        total = sum(jnp.sum(weight.astype(F32) * grad, axis=-1) for weight, grad in pairs)
        return total / gain.astype(F32)

    attn_gain_sum = gain_sum(
        gain_attn,
        (w_query, query_sum),
        (key_projection_weight, key_sum),
        (value_projection_weight, value_sum),
    )
    return (
        output.astype(BF16).reshape(tokens.shape),
        input_grad.astype(BF16).reshape(tokens.shape),
        query_sum,
        key_sum,
        value_sum,
        output_sum,
        gate_sum,
        up_sum,
        down_sum.astype(F32),
        attn_gain_sum,
        query_gain_sum,
        key_gain_sum,
        mlp_gain_sum[:, 0],
    )


def solution(mesh):
    seq = mesh.shape["seq"]
    split = Mesh(mesh.devices.reshape(-1, 2, seq), EVERY)
    rows = P(("outer", "inner"), "seq", None)
    weight = P(EVERY, None)
    gain = P(EVERY)
    return jax.shard_map(
        shards,
        mesh=split,
        in_specs=(rows, P(("outer", "inner"), None), rows) + (weight,) * 7 + (gain,) * 4,
        out_specs=(rows, rows) + (weight,) * 7 + (gain,) * 4,
        check_vma=False,
    )
```

```python
import functools
import jax
import jax.numpy as jnp
from jax import lax
from jax.experimental import pallas as pl
from jax.experimental.pallas import tpu as pltpu
from jax.sharding import Mesh
from jax.sharding import PartitionSpec as P
EPSILON = 1e-06
THETA = 1000000.0
PLANE = ('inner', 'seq')
EVERY = ('outer', 'inner', 'seq')
BF16 = jnp.bfloat16
F32 = jnp.float32
VMEM_LIMIT = 56 * 1024 * 1024
MLP_VMEM_LIMIT = 50 * 1024 * 1024
BUSY = pl.CostEstimate(flops=16 * 10 ** 9, bytes_accessed=10 ** 7, transcendentals=10 ** 6)
CHEAP = pl.CostEstimate(flops=1, bytes_accessed=1, transcendentals=0)

def US(us):
    return pl.CostEstimate(flops=int(us * 10 ** 9) + 1, bytes_accessed=1, transcendentals=0)

def rms_scale(values):
    return lax.rsqrt(jnp.mean(values * values, axis=-1, keepdims=True) + EPSILON)

def norm_back(normalized_grad, normalized, inverse_rms):
    return inverse_rms * (normalized_grad - normalized * jnp.mean(normalized_grad * normalized, axis=-1, keepdims=True))

def after(value, *others):
    if not others:
        return value
    return lax.optimization_barrier((value,) + others)[0]

def plane_routes(outer):

    def pairs(flip):
        out = []
        for o in range(outer):
            for x in range(2):
                for y in range(2):
                    for c in range(2):
                        fx, fy, fc = flip(c)
                        source = ((o * 2 + x) * 2 + y) * 2 + c
                        target = ((o * 2 + (x ^ fx)) * 2 + (y ^ fy)) * 2 + (c ^ fc)
                        out.append((source, target))
        return out
    return (pairs(lambda c: (1, 0, 0) if c == 0 else (0, 1, 0)), pairs(lambda c: (0, 1, 0) if c == 0 else (1, 0, 0)), pairs(lambda c: (0, 0, 1)), pairs(lambda c: (1, 0, 0)))

def plane_gather(block, routes, first_core, *needed):
    route_a, route_b, route_c, _ = routes
    near_a = lax.ppermute(block, EVERY, route_a)
    near_b = lax.ppermute(block, EVERY, route_b)
    near_first = after(near_a, *needed) if needed else near_a
    far = lax.ppermute(near_first, EVERY, route_b)
    here = [block, jnp.where(first_core, near_b, near_a), jnp.where(first_core, near_a, near_b), far]
    blocks = [part for block in here for part in (block, lax.ppermute(block, EVERY, route_c))]
    return (blocks, (near_a, near_b))

def pair_sum(here, other, routes):
    return here.astype(F32) + lax.ppermute(other, EVERY, routes[2]).astype(F32)

class Scatter:
    def __init__(self, routes, first_core):
        self.routes, self.first_core = (routes, first_core)

    def far(self, here, other):
        self.far_sum = pair_sum(here, other, self.routes).astype(BF16)
        self.from_far = lax.ppermute(self.far_sum, EVERY, self.routes[1])
        return self.far_sum

    def row(self, here, other):
        self.row_sum = pair_sum(here, other, self.routes)
        return self.row_sum

    def inner(self, here, other):
        self.inner_sum = pair_sum(here, other, self.routes)
        return self.inner_sum

    def near(self, *needed):
        near_a = jnp.where(self.first_core, self.inner_sum, self.row_sum)
        near_b = jnp.where(self.first_core, self.row_sum, self.inner_sum).astype(BF16)
        self.from_b = lax.ppermute(near_b, EVERY, self.routes[1])
        near_a = (near_a + self.from_far.astype(F32)).astype(BF16)
        if needed:
            near_a = after(near_a, *needed)
        self.from_a = lax.ppermute(near_a, EVERY, self.routes[0])
        return (near_a, near_b)

    def own(self, here, other):
        total = pair_sum(here, other, self.routes)
        return total + self.from_b.astype(F32) + self.from_a.astype(F32)

def plane_scatter(blocks, routes, first_core, *needed, far_needed=()):
    scatter = Scatter(routes, first_core)
    far = blocks[6]
    if far_needed:
        far = after(far, *far_needed)
    scatter.far(far, blocks[7])
    scatter.inner(blocks[4], blocks[5])
    scatter.row(blocks[2], blocks[3])
    scatter.near(*needed)
    total = scatter.own(blocks[0], blocks[1])
    return (total, scatter.from_far, scatter.from_a)

def head_routes(outer, plane, spread):
    routes = []
    for shift in range(outer):
        pairs = []
        for o in range(outer):
            for g in range(plane):
                target = (g + shift) % outer * (plane // spread) + g // spread
                pairs.append((o * plane + g, o * plane + target))
        routes.append(pairs)
    return routes

def heads_gather(rows, head_rows):
    outer, here, width = rows.shape
    plane = lax.axis_size(PLANE)
    me = lax.axis_index(PLANE)
    if plane * head_rows != outer * plane * here or plane * here != head_rows * (plane // outer):
        full = lax.all_gather(rows, PLANE, axis=1, tiled=True).reshape(-1, width)
        return lax.dynamic_slice_in_dim(full, me * head_rows, head_rows)
    arrived = jnp.stack([lax.ppermute(lax.dynamic_index_in_dim(rows, (me + shift) % outer, 0, False), EVERY, route) for shift, route in enumerate(head_routes(outer, plane, outer))])
    slab = me // (plane // outer)
    return jnp.concatenate([lax.dynamic_index_in_dim(arrived, (slab - place) % outer, 0, False) for place in range(outer)])

def head_route(outer, plane):
    return [(n, n % outer * plane + n // outer) for n in range(outer * plane)]

def turn(values):
    return pltpu.roll(values, values.shape[-1] // 2, 1)

def head_forward(projected, gain, cosine, sine):
    scale = rms_scale(projected)
    hat = projected * scale
    scaled = hat * gain
    return (scale, hat, (scaled * cosine + turn(scaled) * sine).astype(BF16))

def head_backward(rotated_grad, gain, scale, hat, cosine, sine):
    grad = rotated_grad * cosine - turn(rotated_grad) * sine
    gain_grad = jnp.sum(grad * hat, axis=0, keepdims=True)
    return (gain_grad, norm_back(grad * gain, hat, scale).astype(BF16))

def matmul(left, right, dims):
    return lax.dot_general(left, right, (dims, ((), ())), preferred_element_type=F32)

def head_probs(query_rot, key_rot, visible):
    head_size = query_rot.shape[-1]
    raw = matmul(query_rot, key_rot, ((1,), (1,))) * head_size ** (-0.5)
    masked = jnp.where(visible, raw, -1e+30)
    exponent = jnp.exp(masked - jnp.max(masked, axis=-1, keepdims=True))
    return exponent / jnp.sum(exponent, axis=-1, keepdims=True)

def visibility(index_row_ref, index_col_ref, start_ref):
    index_row = index_row_ref[...]
    return (index_row >= start_ref[...]) & (index_row <= index_col_ref[...])

def attention_kernel(block_0, block_1, block_2, block_3, gain_attn_ref, w_attn_ref, w_out_ref, cosine_ref, sine_ref, start_ref, index_col_ref, index_row_ref, gain_ref, *refs):
    first = w_attn_ref.ndim == 3
    if first:
        *refs, weight_ref = refs
    normed_ref, projected_ref, mixed_ref = refs[-7:-4]
    out_refs = refs[-4:]
    head_size = cosine_ref.shape[-1]
    length = cosine_ref.shape[0]
    groups = mixed_ref.shape[-1] // head_size
    cosine, sine = (cosine_ref[...], sine_ref[...])
    gain_attn = gain_attn_ref[...]
    if first:
        parts = w_attn_ref.shape[0]
        rows = weight_ref.shape[0] // parts

        @pl.when(pl.program_id(0) == 0)
        def _():
            for at in range(parts):
                weight_ref[at * rows:(at + 1) * rows] = w_attn_ref[at, :rows]
    else:
        weight_ref = w_attn_ref
    for at, block_ref in enumerate((block_0, block_1, block_2, block_3)):
        rows = block_ref[...].astype(F32)
        normed_ref[at // 2, at % 2] = (rows * rms_scale(rows) * gain_attn).astype(BF16)
    normed = normed_ref[...].reshape(length, -1)
    projected = matmul(normed, weight_ref[...], ((1,), (0,)))
    projected_ref[...] = projected.reshape(projected_ref.shape)
    visible = visibility(index_row_ref, index_col_ref, start_ref)
    gain_query, gain_key = (gain_ref[0:1], gain_ref[1:2])
    key_at = groups * head_size
    _, _, key_rot = head_forward(projected[:, key_at:key_at + head_size], gain_key, cosine, sine)
    value = projected[:, key_at + head_size:].astype(BF16)
    heads = []
    for head in range(groups):
        columns = slice(head * head_size, (head + 1) * head_size)
        _, _, query_rot = head_forward(projected[:, columns], gain_query, cosine, sine)
        probs = head_probs(query_rot, key_rot, visible).astype(BF16)
        heads.append(matmul(probs, value, ((1,), (0,))).astype(BF16))
    mixed = jnp.concatenate(heads, axis=1)
    mixed_ref[...] = mixed.reshape(mixed_ref.shape)
    out = matmul(mixed, w_out_ref[...], ((1,), (0,))).astype(BF16)
    rows = length // len(out_refs)
    for at, out_ref in enumerate(out_refs):
        out_ref[...] = out[at * rows:(at + 1) * rows]

def attention_back_kernel(block_0, block_1, block_2, block_3, projected_ref, w_out_ref, cosine_ref, sine_ref, start_ref, index_col_ref, index_row_ref, gain_ref, *refs):
    low_ref, gain_grad_ref = refs[-2:]
    head_size = cosine_ref.shape[-1]
    length = cosine_ref.shape[0]
    groups = w_out_ref.shape[0] // head_size
    factor = head_size ** (-0.5)
    cosine, sine = (cosine_ref[...], sine_ref[...])
    visible = visibility(index_row_ref, index_col_ref, start_ref)
    projected = projected_ref[...].reshape(length, -1)
    out_grad = jnp.concatenate([block_0[...], block_1[...], block_2[...], block_3[...]], axis=0)
    mixed_grad = matmul(out_grad, w_out_ref[...], ((1,), (1,))).astype(BF16)
    gain_query, gain_key = (gain_ref[0:1], gain_ref[1:2])
    key_at = groups * head_size
    key_scale, key_hat, key_rot = head_forward(projected[:, key_at:key_at + head_size], gain_key, cosine, sine)
    value = projected[:, key_at + head_size:].astype(BF16)
    block = low_ref.shape[:-1] + (head_size,)
    key_grad = jnp.zeros((length, head_size), F32)
    value_grad = jnp.zeros((length, head_size), F32)
    query_gain = jnp.zeros((1, head_size), F32)
    for head in range(groups):
        columns = slice(head * head_size, (head + 1) * head_size)
        query_scale, query_hat, query_rot = head_forward(projected[:, columns], gain_query, cosine, sine)
        head_grad = mixed_grad[:, columns]
        probs = head_probs(query_rot, key_rot, visible)
        value_grad += matmul(probs.astype(BF16), head_grad, ((0,), (0,)))
        weighted = probs * matmul(head_grad, value, ((1,), (1,)))
        score_grad = (weighted - probs * jnp.sum(weighted, axis=-1, keepdims=True)).astype(BF16)
        key_grad += matmul(score_grad, query_rot, ((0,), (0,)))
        query_grad = factor * matmul(score_grad, key_rot, ((1,), (0,)))
        gain_part, query_low = head_backward(query_grad, gain_query, query_scale, query_hat, cosine, sine)
        query_gain += gain_part
        low_ref[..., columns] = query_low.reshape(block)
    key_gain, key_low = head_backward(factor * key_grad, gain_key, key_scale, key_hat, cosine, sine)
    low_ref[..., key_at:key_at + head_size] = key_low.reshape(block)
    low_ref[..., key_at + head_size:] = value_grad.astype(BF16).reshape(block)
    gain_grad_ref[...] = jnp.concatenate([query_gain, key_gain, jnp.zeros((6, head_size), F32)], axis=0)

def mlp_forward_kernel(*refs, count):
    chunk_refs = refs[:count]
    w_mlp_ref = refs[count]
    gate_ref, up_ref, hidden_ref, chunk_ref = refs[-4:]
    pair = pl.program_id(0)

    def hold(at):
        chunk_ref[0] = chunk_refs[2 * at][...]
        chunk_ref[1] = chunk_refs[2 * at + 1][...]
    for at in range(count // 2):
        pl.when((pl.program_id(1) == 0) & (pair == at))(functools.partial(hold, at))
    chunk = chunk_ref[...].reshape(-1, chunk_ref.shape[-1])
    step = gate_ref.shape[-1]
    at = pl.multiple_of(pl.program_id(1) * step, step)
    half = w_mlp_ref.shape[1] // 2
    gate = matmul(chunk, w_mlp_ref[:, pl.ds(at, step)], ((1,), (0,)))
    up = matmul(chunk, w_mlp_ref[:, pl.ds(half + at, step)], ((1,), (0,)))
    gate_ref[...] = gate.reshape(gate_ref.shape)
    up_ref[...] = up.reshape(gate_ref.shape)
    hidden_ref[...] = (gate * jax.nn.sigmoid(gate) * up).astype(BF16).reshape(gate_ref.shape)

def mlp_forward(base, chunks, w_mlp, params, cost, *kept):
    count = len(chunks)
    rows, width = chunks[0].shape
    columns = w_mlp.shape[1] // 2
    step = 256 if columns % 256 == 0 else columns
    shape = (8, rows, columns)
    out_spec = pl.BlockSpec((2, rows, step), lambda i, j: (base + i, 0, j))
    return pl.pallas_call(functools.partial(mlp_forward_kernel, count=count), grid=(count // 2, columns // step), in_specs=[pl.BlockSpec((rows, width), lambda i, j: (0, 0))] * count + [pl.BlockSpec(memory_space=pltpu.VMEM)] + [pl.BlockSpec(memory_space=pl.ANY)] * len(kept), out_specs=(out_spec,) * 3 + (pl.BlockSpec((2, rows, width), lambda i, j: (base + i, 0, 0)),), out_shape=(jax.ShapeDtypeStruct(shape, F32), jax.ShapeDtypeStruct(shape, F32), jax.ShapeDtypeStruct(shape, BF16), jax.ShapeDtypeStruct((8, rows, width), BF16)), input_output_aliases={count + 1 + at: at for at in range(len(kept))}, compiler_params=params, cost_estimate=cost)(*chunks, w_mlp, *kept)

def chunk_grad_kernel(left_ref, *refs):
    *chunk_refs, out_ref, turned_ref = refs
    rows = left_ref.shape[1]

    @pl.when(pl.program_id(0) == 0)
    def _():
        for at in range(len(chunk_refs)):
            turned_ref[:, at * rows:(at + 1) * rows] = left_ref[at].T
    right = jnp.concatenate([ref[...] for ref in chunk_refs], axis=0)
    out_ref[...] = matmul(turned_ref[...], right, ((1,), (0,))).astype(BF16)

def chunk_grad(left, chunks, params, cost):
    count, rows, columns = left.shape
    width = chunks[0].shape[1]
    step = 512
    return pl.pallas_call(chunk_grad_kernel, grid=(width // step,), in_specs=[pl.BlockSpec(left.shape, lambda j: (0, 0, 0))] + [pl.BlockSpec((rows, step), lambda j: (0, j))] * count, out_specs=pl.BlockSpec((columns, step), lambda j: (0, j)), out_shape=jax.ShapeDtypeStruct((columns, width), BF16), scratch_shapes=[pltpu.VMEM((columns, count * rows), BF16)], compiler_params=params, cost_estimate=cost)(left, *chunks)

def mlp_backward_kernel(gate_ref, up_ref, w_down_ref, w_mlp_ref, *refs, count):
    cotangent_refs = refs[:count]
    held_ref = refs[-1]
    grad_ref = refs[-count - 2]
    second_refs = refs[-count - 1:-1]
    pair, rows, columns = gate_ref.shape

    def hold(at):
        held_ref[:rows] = cotangent_refs[at][...]
        held_ref[rows:] = cotangent_refs[at + 1][...]
    for at in range(0, count, 2):
        pl.when(pl.program_id(0) == at // 2)(functools.partial(hold, at))
    cotangent = held_ref[...]
    hidden_grad = matmul(cotangent, w_down_ref[...], ((1,), (1,)))
    gate = gate_ref[...].reshape(pair * rows, -1)
    up = up_ref[...].reshape(pair * rows, -1)
    sigma = jax.nn.sigmoid(gate)
    gate_grad = hidden_grad * up * sigma * (1.0 + gate * (1.0 - sigma))
    up_grad = hidden_grad * gate * sigma
    grad = jnp.concatenate([gate_grad.astype(BF16), up_grad.astype(BF16)], axis=1)
    grad_ref[...] = grad.reshape(grad_ref.shape)
    second = matmul(grad, w_mlp_ref[...], ((1,), (1,))).astype(BF16)

    def store(at):
        second_refs[at][...] = second[:rows]
        second_refs[at + 1][...] = second[rows:]
    for at in range(0, count, 2):
        pl.when(pl.program_id(0) == at // 2)(functools.partial(store, at))

def mlp_backward(base, chunks, operands, params, cost, *kept):
    gate = operands[0]
    count = len(chunks)
    rows, width = chunks[0].shape
    columns = gate.shape[-1]

    def pair_spec(last):
        return pl.BlockSpec((2, rows, last), lambda i: (base + i, 0, 0))
    whole = pl.BlockSpec((rows, width), lambda i: (0, 0))
    return pl.pallas_call(functools.partial(mlp_backward_kernel, count=count), grid=(count // 2,), in_specs=[pair_spec(columns)] * 2 + [pl.BlockSpec(memory_space=pltpu.VMEM)] * 2 + [whole] * count + [pl.BlockSpec(memory_space=pl.ANY)] * len(kept), out_specs=(pair_spec(2 * columns),) + (whole,) * count, out_shape=(jax.ShapeDtypeStruct((8, rows, 2 * columns), BF16),) + (jax.ShapeDtypeStruct((rows, width), BF16),) * count, scratch_shapes=[pltpu.VMEM((2 * rows, width), BF16)], input_output_aliases={4 + count + at: at for at in range(len(kept))}, compiler_params=params, cost_estimate=cost)(*operands, *chunks, *kept)

def pack_kernel(gate_ref, up_ref, out_ref, *, step):
    plane, _, columns = out_ref.shape
    hidden = columns // 2
    for g in range(plane):
        for at, ref in enumerate((gate_ref, up_ref)):
            parts = [ref[:, start + g * step:start + (g + 1) * step] for start in range(0, ref.shape[1], plane * step)]
            out_ref[g, :, at * hidden:(at + 1) * hidden] = jnp.concatenate(parts, axis=1)

def unpack_kernel(back_ref, gate_ref, up_ref, gain_ref, gate_out, up_out, gain_out, *, step):
    plane, _, columns = back_ref.shape
    hidden = columns // 2
    total = 0.0
    for at, (weight_ref, out_ref) in enumerate(((gate_ref, gate_out), (up_ref, up_out))):
        parts = [back_ref[g, :, at * hidden + start:at * hidden + start + step] for start in range(0, hidden, step) for g in range(plane)]
        grad = jnp.concatenate(parts, axis=1).astype(F32)
        out_ref[...] = grad
        total += jnp.sum(grad * weight_ref[...].astype(F32), axis=1, keepdims=True)
    gain_out[...] = total / gain_ref[...]

def attn_unpack_kernel(back_ref, *refs):
    weight_refs, gain_ref = (refs[:3], refs[3])
    out_refs, gain_out, line_out = (refs[4:7], refs[7], refs[8])
    plane = back_ref.shape[0]
    rows = gain_ref.shape[0]
    lines, total = (0.0, 0.0)
    for g in range(plane):
        back = back_ref[g].astype(F32)
        lines += back[rows:]
        at = 0
        for weight_ref, out_ref in zip(weight_refs, out_refs, strict=True):
            step = weight_ref.shape[1] // plane
            grad = back[:rows, at:at + step]
            columns = slice(g * step, (g + 1) * step)
            out_ref[:, columns] = grad
            total += jnp.sum(grad * weight_ref[:, columns].astype(F32), axis=1, keepdims=True)
            at += step
    gain_out[...] = total / gain_ref[...]
    line_out[...] = lines

def shards(tokens, segments, cotangent, w_query, key_projection_weight, value_projection_weight, w_output, w_gate, w_up, w_down, gain_attn, gain_query, gain_key, gain_mlp):
    outer = lax.axis_size('outer')
    plane = lax.axis_size('inner') * lax.axis_size('seq')
    local_sequences, local_rows, width = tokens.shape
    total_rows = segments.shape[1]
    rows_here = local_sequences * local_rows
    weight_rows = w_query.shape[0]
    head_size = gain_query.shape[0] * outer * plane
    query_columns = w_query.shape[1] // plane
    key_columns = key_projection_weight.shape[1] // plane
    attn_columns = query_columns + 2 * key_columns
    hidden_rows = w_down.shape[0]
    hidden_columns = hidden_rows * outer
    routes = plane_routes(outer)
    seq_index = lax.axis_index('seq')
    first_core = seq_index % 2 == 0
    tokens_flat = tokens.reshape(rows_here, width)
    segments_there = lax.ppermute(segments, EVERY, routes[3])
    tokens_near = ()
    segments_two = jnp.stack([segments, segments_there])
    core, row = (seq_index % 2, seq_index // 2)
    offsets = jnp.stack([(row ^ r) * 2 + (core ^ c) for r in range(2) for c in range(2)])
    token_index = (offsets[:, None] * local_rows + jnp.arange(local_rows, dtype=jnp.int32)[None]).reshape(-1)
    segments_here = jnp.take(segments_two, token_index, axis=2)
    doc_start = jnp.sum((segments_two[:, :, None, :] < segments_here[:, :, :, None]).astype(jnp.int32), axis=-1)
    positions = (token_index - doc_start).astype(F32)
    half_size = head_size // 2
    frequency = jnp.power(THETA, -(jnp.arange(half_size, dtype=F32) * 2.0 / head_size))
    angles = positions[..., None] * frequency
    cosine, sine = (jnp.cos(angles), jnp.sin(angles))
    cosine = jnp.concatenate([cosine, cosine], axis=-1)
    sine = jnp.concatenate([-sine, sine], axis=-1)
    start_table = doc_start[..., None]
    index_col = token_index[:, None]
    index_row = token_index[None, :]

    def by_column(values):
        return values.reshape(values.shape[0], plane, -1).transpose(1, 0, 2)
    gain_rows = 8
    gain_count = gain_query.shape[0]
    gain_line = jnp.concatenate([gain_attn, gain_mlp, gain_query, gain_key])
    gain_line = jnp.pad(gain_line[None], ((0, gain_rows - 1), (0, attn_columns - gain_line.shape[0])))
    head_pairs = head_route(outer, plane)
    output_rows = lax.all_gather(w_output, 'outer', axis=0)
    attn_send = jnp.concatenate([by_column(w_query), by_column(key_projection_weight), by_column(value_projection_weight)], axis=-1)
    attn_send = jnp.concatenate([attn_send, jnp.broadcast_to(gain_line, (plane,) + gain_line.shape)], axis=1)
    attn_part = lax.all_to_all(attn_send, PLANE, 0, 0, tiled=True)
    ties = ()
    if 0 in (1, 3):
        ties += (output_rows,)
    if 0 in (2, 3):
        ties += tuple(tokens_near)
    attn_full = lax.all_gather(after(attn_part, *ties), 'outer', axis=0, tiled=True)
    gain_lines = attn_full[:, weight_rows]
    at = 0
    gains = []
    for count in (weight_rows, weight_rows, gain_count, gain_count):
        gains.append(gain_lines[:, at:at + count].reshape(-1).astype(F32))
        at += count
    gain_attn_all, gain_mlp_all, gain_query_all, gain_key_all = gains
    head_gains = jnp.concatenate([gain_query_all[None], gain_key_all[None], jnp.zeros((6, head_size), F32)], axis=0)
    params = pltpu.CompilerParams(vmem_limit_bytes=VMEM_LIMIT)
    mlp_send = pl.pallas_call(functools.partial(pack_kernel, step=hidden_rows), out_shape=jax.ShapeDtypeStruct((plane, weight_rows, 2 * hidden_columns), BF16), compiler_params=params, cost_estimate=US(0))(w_gate, w_up)
    w_out = heads_gather(output_rows, query_columns)
    mlp_ties = ()
    mlp_part = lax.all_to_all(after(mlp_send, attn_part, *mlp_ties), PLANE, 0, 0, tiled=True)
    tokens_all, tokens_near = plane_gather(after(tokens_flat, mlp_part), routes, first_core)
    w_mlp = lax.all_gather(mlp_part.reshape(plane * weight_rows, 2 * hidden_columns), 'outer', axis=0, tiled=True)
    blocks = (2, 2, 2, local_sequences, local_rows)
    tables = (cosine, sine, start_table, index_col, index_row, head_gains)

    def whole_spec(value):
        return pl.BlockSpec(value.shape, lambda *at: (0,) * len(value.shape))

    def specs_of(side):
        def token_spec(columns):
            return pl.BlockSpec((None, 2, 2, None, local_rows, columns), lambda *at: (side, 0, 0, at[-1], 0, 0))

        def table_spec(rows, columns):
            return pl.BlockSpec((None, None, rows, columns), lambda *at: (side, at[-1], 0, 0))
        return (token_spec, table_spec, [table_spec(total_rows, head_size), table_spec(total_rows, head_size), table_spec(total_rows, 1), whole_spec(index_col), whole_spec(index_row), whole_spec(head_gains)])
    chunk_spec = pl.BlockSpec((local_rows, width), lambda *at: (at[-1], 0))

    def attention_forward(side, cost, chunks, weight, *kept):
        token_spec, _, table_specs = specs_of(side)
        operands = (*chunks, gain_attn_all[None], weight, w_out) + tables
        clean = (jax.ShapeDtypeStruct((width, attn_columns), BF16),) * (weight.ndim == 3)
        return pl.pallas_call(attention_kernel, grid=(local_sequences,), in_specs=[chunk_spec] * 4 + [pl.BlockSpec((1, width), lambda *at: (0, 0)), whole_spec(weight), whole_spec(w_out)] + table_specs + [pl.BlockSpec(memory_space=pl.ANY)] * len(kept), out_specs=(token_spec(width), token_spec(attn_columns), token_spec(query_columns)) + (chunk_spec,) * 4 + tuple((whole_spec(value) for value in clean)), out_shape=(jax.ShapeDtypeStruct(blocks + (width,), BF16), jax.ShapeDtypeStruct(blocks + (attn_columns,), F32), jax.ShapeDtypeStruct(blocks + (query_columns,), BF16)) + (jax.ShapeDtypeStruct((rows_here, width), BF16),) * 4 + clean, input_output_aliases={len(operands) + at: at for at in range(len(kept))}, compiler_params=params, cost_estimate=cost)(*operands, *kept)

    def attention_backward(side, cost, chunks, *kept):
        token_spec, table_spec, table_specs = specs_of(side)
        operands = (*chunks, projected, w_out) + tables
        return pl.pallas_call(attention_back_kernel, grid=(local_sequences,), in_specs=[chunk_spec] * 4 + [token_spec(attn_columns), whole_spec(w_out)] + table_specs + [pl.BlockSpec(memory_space=pl.ANY)] * len(kept), out_specs=(token_spec(attn_columns), pl.BlockSpec((None, 8, head_size), lambda *at: (at[-1], 0, 0))), out_shape=(jax.ShapeDtypeStruct(blocks + (attn_columns,), BF16), jax.ShapeDtypeStruct((local_sequences, 8, head_size), F32)), input_output_aliases={len(operands) + at: at for at in range(len(kept))}, compiler_params=params, cost_estimate=cost)(*operands, *kept)
    cotangent_flat = cotangent.reshape(rows_here, width)
    cotangent_all, cotangent_near = plane_gather(after(cotangent_flat, w_out, mlp_part, *tokens_all), routes, first_core)
    tokens_all = after(tuple(tokens_all), mlp_part)
    *kept, there_0, there_1, there_2, there_3, w_attn = attention_forward(1, US(0), tokens_all[4:], attn_full)
    scatter = Scatter(routes, first_core)
    far_sum = scatter.far(there_2, there_3)
    inner_sum = scatter.inner(there_0, there_1)
    tokens_own = after(tokens_all, *cotangent_near)
    *kept, here_0, here_1, here_2, here_3 = attention_forward(0, US(14), tokens_own[:4], w_attn, *kept)
    scatter.row(here_2, after(here_3, scatter.from_far))
    scatter.near()
    normed, projected, mixed = kept
    normed = normed.reshape(-1, width)
    mixed = mixed.reshape(-1, query_columns)
    w_down_here = lax.all_gather(after(w_down, mixed), 'outer', axis=0, tiled=True)
    tokens_here = tokens_flat.astype(F32)
    middle = tokens_here + scatter.own(here_0, here_1)
    scale_two = rms_scale(middle)
    hat_two = middle * scale_two
    normed_two, _ = plane_gather((hat_two * gain_mlp_all).astype(BF16), routes, first_core)
    mlp_params = pltpu.CompilerParams(vmem_limit_bytes=MLP_VMEM_LIMIT)
    gate, up, hidden, normed_two = mlp_forward(0, normed_two, w_mlp, mlp_params, US(0))
    normed_two = normed_two.reshape(-1, width)

    def weight_grad(left, right):
        return lax.dot_general(left, right, (((0,), (0,)), ((), ())), preferred_element_type=F32).astype(BF16)

    def times_transposed(left, right):
        return lax.dot_general(left, right, (((1,), (1,)), ((), ())), preferred_element_type=F32)

    def sum_planes(values):
        return lax.psum_scatter(values, 'outer', scatter_dimension=0, tiled=True)
    down_grad = chunk_grad(hidden, cotangent_all, mlp_params, US(14))
    down_sum = sum_planes(down_grad)
    operands = (after(gate, down_grad), up, w_down_here, w_mlp)
    scatter = Scatter(routes, first_core)
    mlp_grad, *far = mlp_backward(3, cotangent_all[6:], operands, mlp_params, US(0))
    far_sum = scatter.far(*far)
    mlp_grad = after(mlp_grad, far_sum)
    mlp_grad, *near = mlp_backward(1, cotangent_all[2:6], operands, mlp_params, US(14), mlp_grad)
    near = after(tuple(near), scatter.from_far)
    scatter.row(*near[:2])
    scatter.inner(*near[2:])
    near_sums = scatter.near()
    mlp_grad, *own = mlp_backward(0, cotangent_all[:2], operands, mlp_params, US(14), mlp_grad)
    mlp_grad = mlp_grad.reshape(-1, 2 * hidden_columns)
    mlp_tie = normed_two
    mlp_part_grad = weight_grad(mlp_tie, mlp_grad)
    mlp_wgrad = sum_planes(after(mlp_part_grad, down_sum))
    down_out = jnp.dot(after(hidden, *own).reshape(-1, hidden_columns), w_down_here, preferred_element_type=F32).astype(BF16)
    second_grad = scatter.own(*own)
    middle_grad = cotangent_flat.astype(F32) + norm_back(after(second_grad, mlp_part_grad) * gain_mlp_all, hat_two, scale_two)
    out_blocks, _ = plane_gather(middle_grad.astype(BF16), routes, first_core)
    output, output_far, output_near = plane_scatter(after(down_out, out_blocks[6]).reshape(plane, rows_here, width), routes, first_core)
    output = middle + output
    mixed_chunks = mixed.reshape(plane, rows_here, query_columns)
    low, gain_here = attention_backward(0, US(14), out_blocks[:4])
    low, gain_there = attention_backward(1, US(14), out_blocks[4:], low)
    low = low.reshape(-1, attn_columns)
    low = after(low, output_far)
    normed_grad = times_transposed(low, w_attn).astype(BF16)
    low = after(low, normed_grad)
    head_gain_grad = jnp.sum(gain_here + gain_there, axis=0)[:2].reshape(-1)
    gain_lines = jnp.zeros((outer, gain_rows, attn_columns), BF16)
    gain_lines = gain_lines.at[:, 0, :2 * head_size].set(jnp.broadcast_to(head_gain_grad.astype(BF16), (outer, 2 * head_size)))
    attn_wgrad = jnp.concatenate([weight_grad(normed, low).reshape(outer, -1, attn_columns), gain_lines], axis=1)
    mlp_back = lax.all_to_all(mlp_wgrad.reshape(plane, weight_rows, 2 * hidden_columns), PLANE, 0, 0, tiled=True)
    normed_low = low
    if 3 in (1, 2):
        normed_low = after(normed_low, attn_wgrad)
    output_wgrad = chunk_grad(after(mixed_chunks, normed_grad, attn_wgrad), out_blocks, params, US(0))
    output_local = output_wgrad
    attn_flat = after(attn_wgrad.reshape(-1, attn_columns), mlp_wgrad)
    attn_wgrad = sum_planes(attn_flat)
    output_wgrad = sum_planes(after(output_wgrad, attn_wgrad))

    def unpack_mlp(mlp_back):
        return pl.pallas_call(functools.partial(unpack_kernel, step=hidden_rows), out_shape=(jax.ShapeDtypeStruct(w_gate.shape, F32), jax.ShapeDtypeStruct(w_up.shape, F32), jax.ShapeDtypeStruct((weight_rows, 1), F32)), compiler_params=params, cost_estimate=US(0))(mlp_back, w_gate, w_up, gain_mlp.astype(F32)[:, None])
    normed_grad = plane_scatter(after(normed_grad, output_near).reshape(plane, rows_here, width), routes, first_core, attn_wgrad, far_needed=())[0]
    attn_rows = attn_wgrad[:plane * weight_rows].reshape(plane, weight_rows, attn_columns)
    gain_send = jnp.broadcast_to(attn_wgrad[plane * weight_rows:], (plane, gain_rows, attn_columns))
    attn_send = jnp.concatenate([attn_rows, gain_send], axis=1)
    attn_back = lax.all_to_all(attn_send, PLANE, 0, 0, tiled=True)
    scale_one = rms_scale(tokens_here)
    input_grad = middle_grad + norm_back(after(normed_grad, attn_back) * gain_attn_all, tokens_here * scale_one, scale_one)
    mlp_back = after(mlp_back, attn_back)
    gate_sum, up_sum, mlp_gain_sum = unpack_mlp(mlp_back)
    attn_back = after(attn_back, output_wgrad)
    query_sum, key_sum, value_sum, attn_gain_sum, head_gain_sum = pl.pallas_call(attn_unpack_kernel, out_shape=(jax.ShapeDtypeStruct(w_query.shape, F32), jax.ShapeDtypeStruct(key_projection_weight.shape, F32), jax.ShapeDtypeStruct(value_projection_weight.shape, F32), jax.ShapeDtypeStruct((weight_rows, 1), F32), jax.ShapeDtypeStruct((gain_rows, attn_columns), F32)), compiler_params=params, cost_estimate=CHEAP)(attn_back, w_query, key_projection_weight, value_projection_weight, gain_attn.astype(F32)[:, None])
    output_sum = lax.ppermute(output_wgrad, EVERY, [(target, source) for source, target in head_pairs]).astype(F32)
    place = lax.axis_index(EVERY) * gain_count
    query_gain_sum = lax.dynamic_slice_in_dim(head_gain_sum[0], place, gain_count)
    key_gain_sum = lax.dynamic_slice_in_dim(head_gain_sum[0], head_size + place, gain_count)
    return (output.astype(BF16).reshape(tokens.shape), input_grad.astype(BF16).reshape(tokens.shape), query_sum, key_sum, value_sum, output_sum, gate_sum, up_sum, down_sum.astype(F32), attn_gain_sum[:, 0], query_gain_sum, key_gain_sum, mlp_gain_sum[:, 0])

def solution(mesh):
    seq = mesh.shape['seq']
    split = Mesh(mesh.devices.reshape(-1, 2, seq), EVERY)
    rows = P(('outer', 'inner'), 'seq', None)
    weight = P(EVERY, None)
    gain = P(EVERY)
    return jax.shard_map(shards, mesh=split, in_specs=(rows, P(('outer', 'inner'), None), rows) + (weight,) * 7 + (gain,) * 4, out_specs=(rows, rows) + (weight,) * 7 + (gain,) * 4, check_vma=False)
```

```python
import functools
import jax
import jax.numpy as jnp
from jax import lax
from jax.experimental import pallas as pl
from jax.experimental.pallas import tpu as pltpu
from jax.sharding import Mesh
from jax.sharding import PartitionSpec as P
EPSILON = 1e-06
THETA = 1000000.0
PLANE = ('inner', 'seq')
EVERY = ('outer', 'inner', 'seq')
BF16 = jnp.bfloat16
F32 = jnp.float32
VMEM_LIMIT = 56 * 1024 * 1024
MLP_VMEM_LIMIT = 50 * 1024 * 1024
CHEAP = pl.CostEstimate(flops=1, bytes_accessed=1, transcendentals=0)

def US(us):
    return pl.CostEstimate(flops=int(us * 10 ** 9) + 1, bytes_accessed=1, transcendentals=0)

def rms_scale(values):
    return lax.rsqrt(jnp.mean(values * values, axis=-1, keepdims=True) + EPSILON)

def norm_back(normalized_grad, normalized, inverse_rms):
    return inverse_rms * (normalized_grad - normalized * jnp.mean(normalized_grad * normalized, axis=-1, keepdims=True))

def after(value, *others):
    if not others:
        return value
    return lax.optimization_barrier((value,) + others)[0]

def plane_routes(outer):

    def pairs(flip):
        out = []
        for o in range(outer):
            for x in range(2):
                for y in range(2):
                    for c in range(2):
                        fx, fy, fc = flip(c)
                        source = ((o * 2 + x) * 2 + y) * 2 + c
                        target = ((o * 2 + (x ^ fx)) * 2 + (y ^ fy)) * 2 + (c ^ fc)
                        out.append((source, target))
        return out
    return (pairs(lambda c: (1, 0, 0) if c == 0 else (0, 1, 0)), pairs(lambda c: (0, 1, 0) if c == 0 else (1, 0, 0)), pairs(lambda c: (0, 0, 1)), pairs(lambda c: (1, 0, 0)))

def plane_gather(block, routes, first_core, *needed):
    route_a, route_b, route_c, _ = routes
    near_a = lax.ppermute(block, EVERY, route_a)
    near_b = lax.ppermute(block, EVERY, route_b)
    near_first = after(near_a, *needed) if needed else near_a
    far = lax.ppermute(near_first, EVERY, route_b)
    here = [block, jnp.where(first_core, near_b, near_a), jnp.where(first_core, near_a, near_b), far]
    blocks = [part for block in here for part in (block, lax.ppermute(block, EVERY, route_c))]
    return (blocks, (near_a, near_b))

def pair_sum(here, other, routes):
    return here.astype(F32) + lax.ppermute(other, EVERY, routes[2]).astype(F32)

class Scatter:
    def __init__(self, routes, first_core):
        self.routes, self.first_core = (routes, first_core)

    def far(self, here, other):
        self.far_sum = pair_sum(here, other, self.routes).astype(BF16)
        self.from_far = lax.ppermute(self.far_sum, EVERY, self.routes[1])
        return self.far_sum

    def row(self, here, other):
        self.row_sum = pair_sum(here, other, self.routes)
        return self.row_sum

    def inner(self, here, other):
        self.inner_sum = pair_sum(here, other, self.routes)
        return self.inner_sum

    def near(self, *needed):
        near_a = jnp.where(self.first_core, self.inner_sum, self.row_sum)
        near_b = jnp.where(self.first_core, self.row_sum, self.inner_sum).astype(BF16)
        self.from_b = lax.ppermute(near_b, EVERY, self.routes[1])
        near_a = (near_a + self.from_far.astype(F32)).astype(BF16)
        if needed:
            near_a = after(near_a, *needed)
        self.from_a = lax.ppermute(near_a, EVERY, self.routes[0])
        return (near_a, near_b)

    def own(self, here, other):
        total = pair_sum(here, other, self.routes)
        return total + self.from_b.astype(F32) + self.from_a.astype(F32)

def plane_scatter(blocks, routes, first_core, *needed, far_needed=()):
    scatter = Scatter(routes, first_core)
    far = blocks[6]
    if far_needed:
        far = after(far, *far_needed)
    scatter.far(far, blocks[7])
    scatter.inner(blocks[4], blocks[5])
    scatter.row(blocks[2], blocks[3])
    scatter.near(*needed)
    total = scatter.own(blocks[0], blocks[1])
    return (total, scatter.from_far, scatter.from_a)

def head_routes(outer, plane, spread):
    routes = []
    for shift in range(outer):
        pairs = []
        for o in range(outer):
            for g in range(plane):
                target = (g + shift) % outer * (plane // spread) + g // spread
                pairs.append((o * plane + g, o * plane + target))
        routes.append(pairs)
    return routes

def heads_gather(rows, head_rows):
    outer, here, width = rows.shape
    plane = lax.axis_size(PLANE)
    me = lax.axis_index(PLANE)
    if plane * head_rows != outer * plane * here or plane * here != head_rows * (plane // outer):
        full = lax.all_gather(rows, PLANE, axis=1, tiled=True).reshape(-1, width)
        return lax.dynamic_slice_in_dim(full, me * head_rows, head_rows)
    arrived = jnp.stack([lax.ppermute(lax.dynamic_index_in_dim(rows, (me + shift) % outer, 0, False), EVERY, route) for shift, route in enumerate(head_routes(outer, plane, outer))])
    slab = me // (plane // outer)
    return jnp.concatenate([lax.dynamic_index_in_dim(arrived, (slab - place) % outer, 0, False) for place in range(outer)])

def head_route(outer, plane):
    return [(n, n % outer * plane + n // outer) for n in range(outer * plane)]

def turn(values):
    return pltpu.roll(values, values.shape[-1] // 2, 1)

def head_forward(projected, gain, cosine, sine):
    scale = rms_scale(projected)
    hat = projected * scale
    scaled = hat * gain
    return (scale, hat, (scaled * cosine + turn(scaled) * sine).astype(BF16))

def head_backward(rotated_grad, gain, scale, hat, cosine, sine):
    grad = rotated_grad * cosine - turn(rotated_grad) * sine
    gain_grad = jnp.sum(grad * hat, axis=0, keepdims=True)
    return (gain_grad, norm_back(grad * gain, hat, scale).astype(BF16))

def matmul(left, right, dims):
    return lax.dot_general(left, right, (dims, ((), ())), preferred_element_type=F32)

def head_probs(query_rot, key_rot, visible):
    head_size = query_rot.shape[-1]
    raw = matmul(query_rot, key_rot, ((1,), (1,))) * head_size ** (-0.5)
    masked = jnp.where(visible, raw, -1e+30)
    exponent = jnp.exp(masked - jnp.max(masked, axis=-1, keepdims=True))
    return exponent / jnp.sum(exponent, axis=-1, keepdims=True)

def visibility(index_row_ref, index_col_ref, start_ref):
    index_row = index_row_ref[...]
    return (index_row >= start_ref[...]) & (index_row <= index_col_ref[...])

def attention_kernel(block_0, block_1, block_2, block_3, gain_attn_ref, w_attn_ref, w_out_ref, cosine_ref, sine_ref, start_ref, index_col_ref, index_row_ref, gain_ref, *refs):
    first = w_attn_ref.ndim == 3
    if first:
        *refs, weight_ref = refs
    normed_ref, projected_ref, mixed_ref = refs[-7:-4]
    out_refs = refs[-4:]
    head_size = cosine_ref.shape[-1]
    length = cosine_ref.shape[0]
    groups = mixed_ref.shape[-1] // head_size
    cosine, sine = (cosine_ref[...], sine_ref[...])
    gain_attn = gain_attn_ref[...]
    if first:
        parts = w_attn_ref.shape[0]
        rows = weight_ref.shape[0] // parts

        @pl.when(pl.program_id(0) == 0)
        def _():
            for at in range(parts):
                weight_ref[at * rows:(at + 1) * rows] = w_attn_ref[at, :rows]
    else:
        weight_ref = w_attn_ref
    for at, block_ref in enumerate((block_0, block_1, block_2, block_3)):
        rows = block_ref[...].astype(F32)
        normed_ref[at // 2, at % 2] = (rows * rms_scale(rows) * gain_attn).astype(BF16)
    normed = normed_ref[...].reshape(length, -1)
    projected = matmul(normed, weight_ref[...], ((1,), (0,)))
    projected_ref[...] = projected.reshape(projected_ref.shape)
    visible = visibility(index_row_ref, index_col_ref, start_ref)
    gain_query, gain_key = (gain_ref[0:1], gain_ref[1:2])
    key_at = groups * head_size
    _, _, key_rot = head_forward(projected[:, key_at:key_at + head_size], gain_key, cosine, sine)
    value = projected[:, key_at + head_size:].astype(BF16)
    heads = []
    for head in range(groups):
        columns = slice(head * head_size, (head + 1) * head_size)
        _, _, query_rot = head_forward(projected[:, columns], gain_query, cosine, sine)
        probs = head_probs(query_rot, key_rot, visible).astype(BF16)
        heads.append(matmul(probs, value, ((1,), (0,))).astype(BF16))
    mixed = jnp.concatenate(heads, axis=1)
    mixed_ref[...] = mixed.reshape(mixed_ref.shape)
    out = matmul(mixed, w_out_ref[...], ((1,), (0,))).astype(BF16)
    rows = length // len(out_refs)
    for at, out_ref in enumerate(out_refs):
        out_ref[...] = out[at * rows:(at + 1) * rows]

def attention_back_kernel(block_0, block_1, block_2, block_3, projected_ref, w_out_ref, cosine_ref, sine_ref, start_ref, index_col_ref, index_row_ref, gain_ref, *refs):
    low_ref, gain_grad_ref = refs[-2:]
    head_size = cosine_ref.shape[-1]
    length = cosine_ref.shape[0]
    groups = w_out_ref.shape[0] // head_size
    factor = head_size ** (-0.5)
    cosine, sine = (cosine_ref[...], sine_ref[...])
    visible = visibility(index_row_ref, index_col_ref, start_ref)
    projected = projected_ref[...].reshape(length, -1)
    out_grad = jnp.concatenate([block_0[...], block_1[...], block_2[...], block_3[...]], axis=0)
    mixed_grad = matmul(out_grad, w_out_ref[...], ((1,), (1,))).astype(BF16)
    gain_query, gain_key = (gain_ref[0:1], gain_ref[1:2])
    key_at = groups * head_size
    key_scale, key_hat, key_rot = head_forward(projected[:, key_at:key_at + head_size], gain_key, cosine, sine)
    value = projected[:, key_at + head_size:].astype(BF16)
    block = low_ref.shape[:-1] + (head_size,)
    key_grad = jnp.zeros((length, head_size), F32)
    value_grad = jnp.zeros((length, head_size), F32)
    query_gain = jnp.zeros((1, head_size), F32)
    for head in range(groups):
        columns = slice(head * head_size, (head + 1) * head_size)
        query_scale, query_hat, query_rot = head_forward(projected[:, columns], gain_query, cosine, sine)
        head_grad = mixed_grad[:, columns]
        probs = head_probs(query_rot, key_rot, visible)
        value_grad += matmul(probs.astype(BF16), head_grad, ((0,), (0,)))
        weighted = probs * matmul(head_grad, value, ((1,), (1,)))
        score_grad = (weighted - probs * jnp.sum(weighted, axis=-1, keepdims=True)).astype(BF16)
        key_grad += matmul(score_grad, query_rot, ((0,), (0,)))
        query_grad = factor * matmul(score_grad, key_rot, ((1,), (0,)))
        gain_part, query_low = head_backward(query_grad, gain_query, query_scale, query_hat, cosine, sine)
        query_gain += gain_part
        low_ref[..., columns] = query_low.reshape(block)
    key_gain, key_low = head_backward(factor * key_grad, gain_key, key_scale, key_hat, cosine, sine)
    low_ref[..., key_at:key_at + head_size] = key_low.reshape(block)
    low_ref[..., key_at + head_size:] = value_grad.astype(BF16).reshape(block)
    gain_grad_ref[...] = jnp.concatenate([query_gain, key_gain, jnp.zeros((6, head_size), F32)], axis=0)

def mlp_forward_kernel(*refs, count):
    chunk_refs = refs[:count]
    w_mlp_ref = refs[count]
    gate_ref, up_ref, hidden_ref, chunk_ref = refs[-4:]
    pair = pl.program_id(0)

    def hold(at):
        chunk_ref[0] = chunk_refs[2 * at][...]
        chunk_ref[1] = chunk_refs[2 * at + 1][...]
    for at in range(count // 2):
        pl.when((pl.program_id(1) == 0) & (pair == at))(functools.partial(hold, at))
    chunk = chunk_ref[...].reshape(-1, chunk_ref.shape[-1])
    half = w_mlp_ref.shape[1] // 2
    gate = matmul(chunk, w_mlp_ref[:, :half], ((1,), (0,)))
    up = matmul(chunk, w_mlp_ref[:, half:], ((1,), (0,)))
    gate_ref[...] = gate.reshape(gate_ref.shape)
    up_ref[...] = up.reshape(gate_ref.shape)
    hidden_ref[...] = (gate * jax.nn.sigmoid(gate) * up).astype(BF16).reshape(gate_ref.shape)

def mlp_forward(base, chunks, w_mlp, params, cost, *kept):
    count = len(chunks)
    rows, width = chunks[0].shape
    columns = w_mlp.shape[1] // 2
    step = columns
    shape = (8, rows, columns)
    out_spec = pl.BlockSpec((2, rows, step), lambda i, j: (base + i, 0, j))
    return pl.pallas_call(functools.partial(mlp_forward_kernel, count=count), grid=(count // 2, columns // step), in_specs=[pl.BlockSpec((rows, width), lambda i, j: (0, 0))] * count + [pl.BlockSpec(memory_space=pltpu.VMEM)] + [pl.BlockSpec(memory_space=pl.ANY)] * len(kept), out_specs=(out_spec,) * 3 + (pl.BlockSpec((2, rows, width), lambda i, j: (base + i, 0, 0)),), out_shape=(jax.ShapeDtypeStruct(shape, F32), jax.ShapeDtypeStruct(shape, F32), jax.ShapeDtypeStruct(shape, BF16), jax.ShapeDtypeStruct((8, rows, width), BF16)), input_output_aliases={count + 1 + at: at for at in range(len(kept))}, compiler_params=params, cost_estimate=cost)(*chunks, w_mlp, *kept)

def chunk_grad_kernel(left_ref, *refs):
    *chunk_refs, out_ref = refs
    total = 0.0
    for at, chunk_ref in enumerate(chunk_refs):
        total += matmul(left_ref[at], chunk_ref[...], ((0,), (0,)))
    out_ref[...] = total.astype(BF16)

def chunk_grad(left, chunks, params, cost):
    count, rows, columns = left.shape
    width = chunks[0].shape[1]
    step = 512
    return pl.pallas_call(chunk_grad_kernel, grid=(width // step,), in_specs=[pl.BlockSpec(left.shape, lambda j: (0, 0, 0))] + [pl.BlockSpec((rows, step), lambda j: (0, j))] * count, out_specs=pl.BlockSpec((columns, step), lambda j: (0, j)), out_shape=jax.ShapeDtypeStruct((columns, width), BF16), compiler_params=params, cost_estimate=cost)(left, *chunks)

def mlp_backward_kernel(gate_ref, up_ref, w_down_ref, w_mlp_ref, *refs, count):
    cotangent_refs = refs[:count]
    held_ref = refs[-1]
    grad_ref = refs[-count - 2]
    second_refs = refs[-count - 1:-1]
    pair, rows, columns = gate_ref.shape

    def hold(at):
        held_ref[:rows] = cotangent_refs[at][...]
        held_ref[rows:] = cotangent_refs[at + 1][...]
    for at in range(0, count, 2):
        pl.when(pl.program_id(0) == at // 2)(functools.partial(hold, at))
    cotangent = held_ref[...]
    hidden_grad = matmul(cotangent, w_down_ref[...], ((1,), (1,)))
    gate = gate_ref[...].reshape(pair * rows, -1)
    up = up_ref[...].reshape(pair * rows, -1)
    sigma = jax.nn.sigmoid(gate)
    gate_grad = hidden_grad * up * sigma * (1.0 + gate * (1.0 - sigma))
    up_grad = hidden_grad * gate * sigma
    grad = jnp.concatenate([gate_grad.astype(BF16), up_grad.astype(BF16)], axis=1)
    grad_ref[...] = grad.reshape(grad_ref.shape)
    second = matmul(grad, w_mlp_ref[...], ((1,), (1,))).astype(BF16)

    def store(at):
        second_refs[at][...] = second[:rows]
        second_refs[at + 1][...] = second[rows:]
    for at in range(0, count, 2):
        pl.when(pl.program_id(0) == at // 2)(functools.partial(store, at))

def mlp_backward(base, chunks, operands, params, cost, *kept):
    gate = operands[0]
    count = len(chunks)
    rows, width = chunks[0].shape
    columns = gate.shape[-1]

    def pair_spec(last):
        return pl.BlockSpec((2, rows, last), lambda i: (base + i, 0, 0))
    whole = pl.BlockSpec((rows, width), lambda i: (0, 0))
    return pl.pallas_call(functools.partial(mlp_backward_kernel, count=count), grid=(count // 2,), in_specs=[pair_spec(columns)] * 2 + [pl.BlockSpec(memory_space=pltpu.VMEM)] * 2 + [whole] * count + [pl.BlockSpec(memory_space=pl.ANY)] * len(kept), out_specs=(pair_spec(2 * columns),) + (whole,) * count, out_shape=(jax.ShapeDtypeStruct((8, rows, 2 * columns), BF16),) + (jax.ShapeDtypeStruct((rows, width), BF16),) * count, scratch_shapes=[pltpu.VMEM((2 * rows, width), BF16)], input_output_aliases={4 + count + at: at for at in range(len(kept))}, compiler_params=params, cost_estimate=cost)(*operands, *chunks, *kept)

def pack_kernel(gate_ref, up_ref, out_ref, *, step):
    plane, _, columns = out_ref.shape
    hidden = columns // 2
    for g in range(plane):
        for at, ref in enumerate((gate_ref, up_ref)):
            parts = [ref[:, start + g * step:start + (g + 1) * step] for start in range(0, ref.shape[1], plane * step)]
            out_ref[g, :, at * hidden:(at + 1) * hidden] = jnp.concatenate(parts, axis=1)

def unpack_kernel(back_ref, gate_ref, up_ref, gain_ref, gate_out, up_out, gain_out, *, step):
    plane, _, columns = back_ref.shape
    hidden = columns // 2
    total = 0.0
    for at, (weight_ref, out_ref) in enumerate(((gate_ref, gate_out), (up_ref, up_out))):
        parts = [back_ref[g, :, at * hidden + start:at * hidden + start + step] for start in range(0, hidden, step) for g in range(plane)]
        grad = jnp.concatenate(parts, axis=1).astype(F32)
        out_ref[...] = grad
        total += jnp.sum(grad * weight_ref[...].astype(F32), axis=1, keepdims=True)
    gain_out[...] = total / gain_ref[...]

def attn_unpack_kernel(back_ref, *refs):
    weight_refs, gain_ref = (refs[:3], refs[3])
    out_refs, gain_out, line_out = (refs[4:7], refs[7], refs[8])
    plane = back_ref.shape[0]
    rows = gain_ref.shape[0]
    lines, total = (0.0, 0.0)
    for g in range(plane):
        back = back_ref[g].astype(F32)
        lines += back[rows:]
        at = 0
        for weight_ref, out_ref in zip(weight_refs, out_refs, strict=True):
            step = weight_ref.shape[1] // plane
            grad = back[:rows, at:at + step]
            columns = slice(g * step, (g + 1) * step)
            out_ref[:, columns] = grad
            total += jnp.sum(grad * weight_ref[:, columns].astype(F32), axis=1, keepdims=True)
            at += step
    gain_out[...] = total / gain_ref[...]
    line_out[...] = lines

def shards(tokens, segments, cotangent, w_query, key_projection_weight, value_projection_weight, w_output, w_gate, w_up, w_down, gain_attn, gain_query, gain_key, gain_mlp):
    outer = lax.axis_size('outer')
    plane = lax.axis_size('inner') * lax.axis_size('seq')
    local_sequences, local_rows, width = tokens.shape
    total_rows = segments.shape[1]
    rows_here = local_sequences * local_rows
    weight_rows = w_query.shape[0]
    head_size = gain_query.shape[0] * outer * plane
    query_columns = w_query.shape[1] // plane
    key_columns = key_projection_weight.shape[1] // plane
    attn_columns = query_columns + 2 * key_columns
    hidden_rows = w_down.shape[0]
    hidden_columns = hidden_rows * outer
    routes = plane_routes(outer)
    seq_index = lax.axis_index('seq')
    first_core = seq_index % 2 == 0
    tokens_flat = tokens.reshape(rows_here, width)
    segments_there = lax.ppermute(segments, EVERY, routes[3])
    tokens_near = ()
    segments_two = jnp.stack([segments, segments_there])
    core, row = (seq_index % 2, seq_index // 2)
    offsets = jnp.stack([(row ^ r) * 2 + (core ^ c) for r in range(2) for c in range(2)])
    token_index = (offsets[:, None] * local_rows + jnp.arange(local_rows, dtype=jnp.int32)[None]).reshape(-1)
    segments_here = jnp.take(segments_two, token_index, axis=2)
    doc_start = jnp.sum((segments_two[:, :, None, :] < segments_here[:, :, :, None]).astype(jnp.int32), axis=-1)
    positions = (token_index - doc_start).astype(F32)
    half_size = head_size // 2
    frequency = jnp.power(THETA, -(jnp.arange(half_size, dtype=F32) * 2.0 / head_size))
    angles = positions[..., None] * frequency
    cosine, sine = (jnp.cos(angles), jnp.sin(angles))
    cosine = jnp.concatenate([cosine, cosine], axis=-1)
    sine = jnp.concatenate([-sine, sine], axis=-1)
    start_table = doc_start[..., None]
    index_col = token_index[:, None]
    index_row = token_index[None, :]

    def by_column(values):
        return values.reshape(values.shape[0], plane, -1).transpose(1, 0, 2)
    gain_rows = 8
    gain_count = gain_query.shape[0]
    gain_line = jnp.concatenate([gain_attn, gain_mlp, gain_query, gain_key])
    gain_line = jnp.pad(gain_line[None], ((0, gain_rows - 1), (0, attn_columns - gain_line.shape[0])))
    head_pairs = head_route(outer, plane)
    output_rows = lax.all_gather(w_output, 'outer', axis=0)
    attn_send = jnp.concatenate([by_column(w_query), by_column(key_projection_weight), by_column(value_projection_weight)], axis=-1)
    attn_send = jnp.concatenate([attn_send, jnp.broadcast_to(gain_line, (plane,) + gain_line.shape)], axis=1)
    attn_part = lax.all_to_all(attn_send, PLANE, 0, 0, tiled=True)
    ties = ()
    if 0 in (1, 3):
        ties += (output_rows,)
    if 0 in (2, 3):
        ties += tuple(tokens_near)
    attn_full = lax.all_gather(after(attn_part, *ties), 'outer', axis=0, tiled=True)
    gain_lines = attn_full[:, weight_rows]
    at = 0
    gains = []
    for count in (weight_rows, weight_rows, gain_count, gain_count):
        gains.append(gain_lines[:, at:at + count].reshape(-1).astype(F32))
        at += count
    gain_attn_all, gain_mlp_all, gain_query_all, gain_key_all = gains
    head_gains = jnp.concatenate([gain_query_all[None], gain_key_all[None], jnp.zeros((6, head_size), F32)], axis=0)
    params = pltpu.CompilerParams(vmem_limit_bytes=VMEM_LIMIT)
    mlp_send = pl.pallas_call(functools.partial(pack_kernel, step=hidden_rows), out_shape=jax.ShapeDtypeStruct((plane, weight_rows, 2 * hidden_columns), BF16), compiler_params=params, cost_estimate=US(0))(w_gate, w_up)
    w_out = heads_gather(output_rows, query_columns)
    mlp_ties = ()
    mlp_part = lax.all_to_all(after(mlp_send, attn_part, *mlp_ties), PLANE, 0, 0, tiled=True)
    tokens_all, tokens_near = plane_gather(after(tokens_flat, mlp_part), routes, first_core)
    w_mlp = lax.all_gather(mlp_part.reshape(plane * weight_rows, 2 * hidden_columns), 'outer', axis=0, tiled=True)
    blocks = (2, 2, 2, local_sequences, local_rows)
    tables = (cosine, sine, start_table, index_col, index_row, head_gains)

    def whole_spec(value):
        return pl.BlockSpec(value.shape, lambda *at: (0,) * len(value.shape))

    def specs_of(side):
        def token_spec(columns):
            return pl.BlockSpec((None, 2, 2, None, local_rows, columns), lambda *at: (side, 0, 0, at[-1], 0, 0))

        def table_spec(rows, columns):
            return pl.BlockSpec((None, None, rows, columns), lambda *at: (side, at[-1], 0, 0))
        return (token_spec, table_spec, [table_spec(total_rows, head_size), table_spec(total_rows, head_size), table_spec(total_rows, 1), whole_spec(index_col), whole_spec(index_row), whole_spec(head_gains)])
    chunk_spec = pl.BlockSpec((local_rows, width), lambda *at: (at[-1], 0))

    def attention_forward(side, cost, chunks, weight, *kept):
        token_spec, _, table_specs = specs_of(side)
        operands = (*chunks, gain_attn_all[None], weight, w_out) + tables
        clean = (jax.ShapeDtypeStruct((width, attn_columns), BF16),) * (weight.ndim == 3)
        return pl.pallas_call(attention_kernel, grid=(local_sequences,), in_specs=[chunk_spec] * 4 + [pl.BlockSpec((1, width), lambda *at: (0, 0)), whole_spec(weight), whole_spec(w_out)] + table_specs + [pl.BlockSpec(memory_space=pl.ANY)] * len(kept), out_specs=(token_spec(width), token_spec(attn_columns), token_spec(query_columns)) + (chunk_spec,) * 4 + tuple((whole_spec(value) for value in clean)), out_shape=(jax.ShapeDtypeStruct(blocks + (width,), BF16), jax.ShapeDtypeStruct(blocks + (attn_columns,), F32), jax.ShapeDtypeStruct(blocks + (query_columns,), BF16)) + (jax.ShapeDtypeStruct((rows_here, width), BF16),) * 4 + clean, input_output_aliases={len(operands) + at: at for at in range(len(kept))}, compiler_params=params, cost_estimate=cost)(*operands, *kept)

    def attention_backward(side, cost, chunks, *kept):
        token_spec, table_spec, table_specs = specs_of(side)
        operands = (*chunks, projected, w_out) + tables
        return pl.pallas_call(attention_back_kernel, grid=(local_sequences,), in_specs=[chunk_spec] * 4 + [token_spec(attn_columns), whole_spec(w_out)] + table_specs + [pl.BlockSpec(memory_space=pl.ANY)] * len(kept), out_specs=(token_spec(attn_columns), pl.BlockSpec((None, 8, head_size), lambda *at: (at[-1], 0, 0))), out_shape=(jax.ShapeDtypeStruct(blocks + (attn_columns,), BF16), jax.ShapeDtypeStruct((local_sequences, 8, head_size), F32)), input_output_aliases={len(operands) + at: at for at in range(len(kept))}, compiler_params=params, cost_estimate=cost)(*operands, *kept)
    cotangent_flat = cotangent.reshape(rows_here, width)
    cotangent_all, cotangent_near = plane_gather(after(cotangent_flat, w_out, mlp_part, *tokens_all), routes, first_core)
    tokens_all = after(tuple(tokens_all), mlp_part)
    *kept, there_0, there_1, there_2, there_3, w_attn = attention_forward(1, US(0), tokens_all[4:], attn_full)
    scatter = Scatter(routes, first_core)
    far_sum = scatter.far(there_2, there_3)
    inner_sum = scatter.inner(there_0, there_1)
    tokens_own = after(tokens_all, *cotangent_near)
    *kept, here_0, here_1, here_2, here_3 = attention_forward(0, US(14), tokens_own[:4], w_attn, *kept)
    scatter.row(here_2, after(here_3, scatter.from_far))
    scatter.near()
    normed, projected, mixed = kept
    normed = normed.reshape(-1, width)
    mixed = mixed.reshape(-1, query_columns)
    w_down_here = lax.all_gather(after(w_down, mixed), 'outer', axis=0, tiled=True)
    tokens_here = tokens_flat.astype(F32)
    middle = tokens_here + scatter.own(here_0, here_1)
    scale_two = rms_scale(middle)
    hat_two = middle * scale_two
    normed_two, _ = plane_gather((hat_two * gain_mlp_all).astype(BF16), routes, first_core)
    mlp_params = pltpu.CompilerParams(vmem_limit_bytes=MLP_VMEM_LIMIT)
    gate, up, hidden, normed_two = mlp_forward(0, normed_two, w_mlp, mlp_params, US(0))
    normed_two = normed_two.reshape(-1, width)

    def weight_grad(left, right):
        return lax.dot_general(left, right, (((0,), (0,)), ((), ())), preferred_element_type=F32).astype(BF16)

    def times_transposed(left, right):
        return lax.dot_general(left, right, (((1,), (1,)), ((), ())), preferred_element_type=F32)

    def sum_planes(values):
        return lax.psum_scatter(values, 'outer', scatter_dimension=0, tiled=True)
    down_grad = chunk_grad(hidden, cotangent_all, mlp_params, US(6))
    down_sum = sum_planes(down_grad)
    operands = (after(gate, down_grad), up, w_down_here, w_mlp)
    scatter = Scatter(routes, first_core)
    mlp_grad, *far = mlp_backward(3, cotangent_all[6:], operands, mlp_params, US(0))
    far_sum = scatter.far(*far)
    mlp_grad = after(mlp_grad, far_sum)
    mlp_grad, *near = mlp_backward(1, cotangent_all[2:6], operands, mlp_params, US(14), mlp_grad)
    near = after(tuple(near), scatter.from_far)
    scatter.row(*near[:2])
    scatter.inner(*near[2:])
    near_sums = scatter.near()
    mlp_grad, *own = mlp_backward(0, cotangent_all[:2], operands, mlp_params, US(14), mlp_grad)
    mlp_grad = mlp_grad.reshape(-1, 2 * hidden_columns)
    mlp_tie = normed_two
    mlp_tie = after(mlp_tie, near_sums[1])
    mlp_part_grad = weight_grad(mlp_tie, mlp_grad)
    mlp_wgrad = sum_planes(after(mlp_part_grad, down_sum))
    down_out = jnp.dot(after(hidden, *own).reshape(-1, hidden_columns), w_down_here, preferred_element_type=F32).astype(BF16)
    second_grad = scatter.own(*own)
    middle_grad = cotangent_flat.astype(F32) + norm_back(after(second_grad, mlp_part_grad) * gain_mlp_all, hat_two, scale_two)
    out_blocks, _ = plane_gather(middle_grad.astype(BF16), routes, first_core)
    output, output_far, output_near = plane_scatter(after(down_out, out_blocks[6]).reshape(plane, rows_here, width), routes, first_core)
    output = middle + output
    mixed_chunks = mixed.reshape(plane, rows_here, query_columns)
    low, gain_here = attention_backward(0, US(14), out_blocks[:4])
    low, gain_there = attention_backward(1, US(14), out_blocks[4:], low)
    low = low.reshape(-1, attn_columns)
    low = after(low, output_far)
    normed_grad = times_transposed(low, w_attn).astype(BF16)
    low = after(low, normed_grad)
    head_gain_grad = jnp.sum(gain_here + gain_there, axis=0)[:2].reshape(-1)
    gain_lines = jnp.zeros((outer, gain_rows, attn_columns), BF16)
    gain_lines = gain_lines.at[:, 0, :2 * head_size].set(jnp.broadcast_to(head_gain_grad.astype(BF16), (outer, 2 * head_size)))
    attn_wgrad = jnp.concatenate([weight_grad(normed, low).reshape(outer, -1, attn_columns), gain_lines], axis=1)
    mlp_back = lax.all_to_all(mlp_wgrad.reshape(plane, weight_rows, 2 * hidden_columns), PLANE, 0, 0, tiled=True)
    normed_low = low
    if 3 in (1, 2):
        normed_low = after(normed_low, attn_wgrad)
    output_wgrad = chunk_grad(after(mixed_chunks, normed_grad, attn_wgrad), out_blocks, params, US(0))
    output_local = output_wgrad
    attn_flat = after(attn_wgrad.reshape(-1, attn_columns), mlp_wgrad)
    attn_wgrad = sum_planes(attn_flat)
    output_wgrad = sum_planes(after(output_wgrad, attn_wgrad))

    def unpack_mlp(mlp_back):
        return pl.pallas_call(functools.partial(unpack_kernel, step=hidden_rows), out_shape=(jax.ShapeDtypeStruct(w_gate.shape, F32), jax.ShapeDtypeStruct(w_up.shape, F32), jax.ShapeDtypeStruct((weight_rows, 1), F32)), compiler_params=params, cost_estimate=US(0))(mlp_back, w_gate, w_up, gain_mlp.astype(F32)[:, None])
    normed_grad = plane_scatter(after(normed_grad, output_near).reshape(plane, rows_here, width), routes, first_core, attn_wgrad, far_needed=())[0]
    attn_rows = attn_wgrad[:plane * weight_rows].reshape(plane, weight_rows, attn_columns)
    gain_send = jnp.broadcast_to(attn_wgrad[plane * weight_rows:], (plane, gain_rows, attn_columns))
    attn_send = jnp.concatenate([attn_rows, gain_send], axis=1)
    attn_back = lax.all_to_all(attn_send, PLANE, 0, 0, tiled=True)
    scale_one = rms_scale(tokens_here)
    input_grad = middle_grad + norm_back(after(normed_grad, attn_back) * gain_attn_all, tokens_here * scale_one, scale_one)
    mlp_back = after(mlp_back, attn_back)
    gate_sum, up_sum, mlp_gain_sum = unpack_mlp(mlp_back)
    attn_back = after(attn_back, output_wgrad)
    query_sum, key_sum, value_sum, attn_gain_sum, head_gain_sum = pl.pallas_call(attn_unpack_kernel, out_shape=(jax.ShapeDtypeStruct(w_query.shape, F32), jax.ShapeDtypeStruct(key_projection_weight.shape, F32), jax.ShapeDtypeStruct(value_projection_weight.shape, F32), jax.ShapeDtypeStruct((weight_rows, 1), F32), jax.ShapeDtypeStruct((gain_rows, attn_columns), F32)), compiler_params=params, cost_estimate=CHEAP)(attn_back, w_query, key_projection_weight, value_projection_weight, gain_attn.astype(F32)[:, None])
    output_sum = lax.ppermute(output_wgrad, EVERY, [(target, source) for source, target in head_pairs]).astype(F32)
    place = lax.axis_index(EVERY) * gain_count
    query_gain_sum = lax.dynamic_slice_in_dim(head_gain_sum[0], place, gain_count)
    key_gain_sum = lax.dynamic_slice_in_dim(head_gain_sum[0], head_size + place, gain_count)
    return (output.astype(BF16).reshape(tokens.shape), input_grad.astype(BF16).reshape(tokens.shape), query_sum, key_sum, value_sum, output_sum, gate_sum, up_sum, down_sum.astype(F32), attn_gain_sum[:, 0], query_gain_sum, key_gain_sum, mlp_gain_sum[:, 0])

def solution(mesh):
    seq = mesh.shape['seq']
    split = Mesh(mesh.devices.reshape(-1, 2, seq), EVERY)
    rows = P(('outer', 'inner'), 'seq', None)
    weight = P(EVERY, None)
    gain = P(EVERY)
    return jax.shard_map(shards, mesh=split, in_specs=(rows, P(('outer', 'inner'), None), rows) + (weight,) * 7 + (gain,) * 4, out_specs=(rows, rows) + (weight,) * 7 + (gain,) * 4, check_vma=False)
```

```python
import functools
import jax
import jax.numpy as jnp
from jax import lax
from jax.experimental import pallas as pl
from jax.experimental.pallas import tpu as pltpu
from jax.sharding import Mesh
from jax.sharding import PartitionSpec as P
EPSILON = 1e-06
THETA = 1000000.0
PLANE = ('inner', 'seq')
EVERY = ('outer', 'inner', 'seq')
BF16 = jnp.bfloat16
F32 = jnp.float32
VMEM_LIMIT = 56 * 1024 * 1024
MLP_VMEM_LIMIT = 50 * 1024 * 1024
CHEAP = pl.CostEstimate(flops=1, bytes_accessed=1, transcendentals=0)

def US(us):
    return pl.CostEstimate(flops=int(us * 10 ** 9) + 1, bytes_accessed=1, transcendentals=0)

def rms_scale(values):
    return lax.rsqrt(jnp.mean(values * values, axis=-1, keepdims=True) + EPSILON)

def norm_back(normalized_grad, normalized, inverse_rms):
    return inverse_rms * (normalized_grad - normalized * jnp.mean(normalized_grad * normalized, axis=-1, keepdims=True))

def after(value, *others):
    if not others:
        return value
    return lax.optimization_barrier((value,) + others)[0]

def plane_routes(outer):

    def pairs(flip):
        out = []
        for o in range(outer):
            for x in range(2):
                for y in range(2):
                    for c in range(2):
                        fx, fy, fc = flip(c)
                        source = ((o * 2 + x) * 2 + y) * 2 + c
                        target = ((o * 2 + (x ^ fx)) * 2 + (y ^ fy)) * 2 + (c ^ fc)
                        out.append((source, target))
        return out
    return (pairs(lambda c: (1, 0, 0) if c == 0 else (0, 1, 0)), pairs(lambda c: (0, 1, 0) if c == 0 else (1, 0, 0)), pairs(lambda c: (0, 0, 1)), pairs(lambda c: (1, 0, 0)))

def plane_gather(block, routes, first_core, *needed):
    route_a, route_b, route_c, _ = routes
    near_a = lax.ppermute(block, EVERY, route_a)
    near_b = lax.ppermute(block, EVERY, route_b)
    near_first = after(near_a, *needed) if needed else near_a
    far = lax.ppermute(near_first, EVERY, route_b)
    here = [block, jnp.where(first_core, near_b, near_a), jnp.where(first_core, near_a, near_b), far]
    blocks = [part for block in here for part in (block, lax.ppermute(block, EVERY, route_c))]
    return (blocks, (near_a, near_b))

def pair_sum(here, other, routes):
    return here.astype(F32) + lax.ppermute(other, EVERY, routes[2]).astype(F32)

class Scatter:
    def __init__(self, routes, first_core):
        self.routes, self.first_core = (routes, first_core)

    def far(self, here, other):
        self.far_sum = pair_sum(here, other, self.routes).astype(BF16)
        self.from_far = lax.ppermute(self.far_sum, EVERY, self.routes[1])
        return self.far_sum

    def row(self, here, other):
        self.row_sum = pair_sum(here, other, self.routes)
        return self.row_sum

    def inner(self, here, other):
        self.inner_sum = pair_sum(here, other, self.routes)
        return self.inner_sum

    def near(self, *needed):
        near_a = jnp.where(self.first_core, self.inner_sum, self.row_sum)
        near_b = jnp.where(self.first_core, self.row_sum, self.inner_sum).astype(BF16)
        self.from_b = lax.ppermute(near_b, EVERY, self.routes[1])
        near_a = (near_a + self.from_far.astype(F32)).astype(BF16)
        if needed:
            near_a = after(near_a, *needed)
        self.from_a = lax.ppermute(near_a, EVERY, self.routes[0])
        return (near_a, near_b)

    def own(self, here, other):
        total = pair_sum(here, other, self.routes)
        return total + self.from_b.astype(F32) + self.from_a.astype(F32)

def plane_scatter(blocks, routes, first_core, *needed, far_needed=()):
    scatter = Scatter(routes, first_core)
    far = blocks[6]
    if far_needed:
        far = after(far, *far_needed)
    scatter.far(far, blocks[7])
    scatter.inner(blocks[4], blocks[5])
    scatter.row(blocks[2], blocks[3])
    scatter.near(*needed)
    total = scatter.own(blocks[0], blocks[1])
    return (total, scatter.from_far, scatter.from_a)

def head_routes(outer, plane, spread):
    routes = []
    for shift in range(outer):
        pairs = []
        for o in range(outer):
            for g in range(plane):
                target = (g + shift) % outer * (plane // spread) + g // spread
                pairs.append((o * plane + g, o * plane + target))
        routes.append(pairs)
    return routes

def heads_gather(rows, head_rows):
    outer, here, width = rows.shape
    plane = lax.axis_size(PLANE)
    me = lax.axis_index(PLANE)
    if plane * head_rows != outer * plane * here or plane * here != head_rows * (plane // outer):
        full = lax.all_gather(rows, PLANE, axis=1, tiled=True).reshape(-1, width)
        return lax.dynamic_slice_in_dim(full, me * head_rows, head_rows)
    arrived = jnp.stack([lax.ppermute(lax.dynamic_index_in_dim(rows, (me + shift) % outer, 0, False), EVERY, route) for shift, route in enumerate(head_routes(outer, plane, outer))])
    slab = me // (plane // outer)
    return jnp.concatenate([lax.dynamic_index_in_dim(arrived, (slab - place) % outer, 0, False) for place in range(outer)])

def head_route(outer, plane):
    return [(n, n % outer * plane + n // outer) for n in range(outer * plane)]

def turn(values):
    return pltpu.roll(values, values.shape[-1] // 2, 1)

def head_forward(projected, gain, cosine, sine):
    scale = rms_scale(projected)
    hat = projected * scale
    scaled = hat * gain
    return (scale, hat, (scaled * cosine + turn(scaled) * sine).astype(BF16))

def head_backward(rotated_grad, gain, scale, hat, cosine, sine):
    grad = rotated_grad * cosine - turn(rotated_grad) * sine
    gain_grad = jnp.sum(grad * hat, axis=0, keepdims=True)
    return (gain_grad, norm_back(grad * gain, hat, scale).astype(BF16))

def matmul(left, right, dims):
    return lax.dot_general(left, right, (dims, ((), ())), preferred_element_type=F32)

def head_probs(query_rot, key_rot, visible):
    head_size = query_rot.shape[-1]
    raw = matmul(query_rot, key_rot, ((1,), (1,))) * head_size ** (-0.5)
    masked = jnp.where(visible, raw, -1e+30)
    exponent = jnp.exp(masked - jnp.max(masked, axis=-1, keepdims=True))
    return exponent / jnp.sum(exponent, axis=-1, keepdims=True)

def visibility(index_row_ref, index_col_ref, start_ref):
    index_row = index_row_ref[...]
    return (index_row >= start_ref[...]) & (index_row <= index_col_ref[...])

def attention_kernel(block_0, block_1, block_2, block_3, gain_attn_ref, w_attn_ref, w_out_ref, cosine_ref, sine_ref, start_ref, index_col_ref, index_row_ref, gain_ref, *refs):
    first = w_attn_ref.ndim == 3
    if first:
        *refs, weight_ref = refs
    normed_ref, projected_ref, mixed_ref = refs[-7:-4]
    out_refs = refs[-4:]
    head_size = cosine_ref.shape[-1]
    length = cosine_ref.shape[0]
    groups = mixed_ref.shape[-1] // head_size
    cosine, sine = (cosine_ref[...], sine_ref[...])
    gain_attn = gain_attn_ref[...]
    if first:
        parts = w_attn_ref.shape[0]
        rows = weight_ref.shape[0] // parts

        @pl.when(pl.program_id(0) == 0)
        def _():
            for at in range(parts):
                weight_ref[at * rows:(at + 1) * rows] = w_attn_ref[at, :rows]
    else:
        weight_ref = w_attn_ref
    for at, block_ref in enumerate((block_0, block_1, block_2, block_3)):
        rows = block_ref[...].astype(F32)
        normed_ref[at // 2, at % 2] = (rows * rms_scale(rows) * gain_attn).astype(BF16)
    normed = normed_ref[...].reshape(length, -1)
    projected = matmul(normed, weight_ref[...], ((1,), (0,)))
    projected_ref[...] = projected.reshape(projected_ref.shape)
    visible = visibility(index_row_ref, index_col_ref, start_ref)
    gain_query, gain_key = (gain_ref[0:1], gain_ref[1:2])
    key_at = groups * head_size
    _, _, key_rot = head_forward(projected[:, key_at:key_at + head_size], gain_key, cosine, sine)
    value = projected[:, key_at + head_size:].astype(BF16)
    heads = []
    for head in range(groups):
        columns = slice(head * head_size, (head + 1) * head_size)
        _, _, query_rot = head_forward(projected[:, columns], gain_query, cosine, sine)
        probs = head_probs(query_rot, key_rot, visible).astype(BF16)
        heads.append(matmul(probs, value, ((1,), (0,))).astype(BF16))
    mixed = jnp.concatenate(heads, axis=1)
    mixed_ref[...] = mixed.reshape(mixed_ref.shape)
    out = matmul(mixed, w_out_ref[...], ((1,), (0,))).astype(BF16)
    rows = length // len(out_refs)
    for at, out_ref in enumerate(out_refs):
        out_ref[...] = out[at * rows:(at + 1) * rows]

def attention_back_kernel(block_0, block_1, block_2, block_3, projected_ref, w_out_ref, cosine_ref, sine_ref, start_ref, index_col_ref, index_row_ref, gain_ref, *refs):
    low_ref, gain_grad_ref = refs[-2:]
    head_size = cosine_ref.shape[-1]
    length = cosine_ref.shape[0]
    groups = w_out_ref.shape[0] // head_size
    factor = head_size ** (-0.5)
    cosine, sine = (cosine_ref[...], sine_ref[...])
    visible = visibility(index_row_ref, index_col_ref, start_ref)
    projected = projected_ref[...].reshape(length, -1)
    out_grad = jnp.concatenate([block_0[...], block_1[...], block_2[...], block_3[...]], axis=0)
    mixed_grad = matmul(out_grad, w_out_ref[...], ((1,), (1,))).astype(BF16)
    gain_query, gain_key = (gain_ref[0:1], gain_ref[1:2])
    key_at = groups * head_size
    key_scale, key_hat, key_rot = head_forward(projected[:, key_at:key_at + head_size], gain_key, cosine, sine)
    value = projected[:, key_at + head_size:].astype(BF16)
    block = low_ref.shape[:-1] + (head_size,)
    key_grad = jnp.zeros((length, head_size), F32)
    value_grad = jnp.zeros((length, head_size), F32)
    query_gain = jnp.zeros((1, head_size), F32)
    for head in range(groups):
        columns = slice(head * head_size, (head + 1) * head_size)
        query_scale, query_hat, query_rot = head_forward(projected[:, columns], gain_query, cosine, sine)
        head_grad = mixed_grad[:, columns]
        probs = head_probs(query_rot, key_rot, visible)
        value_grad += matmul(probs.astype(BF16), head_grad, ((0,), (0,)))
        weighted = probs * matmul(head_grad, value, ((1,), (1,)))
        score_grad = (weighted - probs * jnp.sum(weighted, axis=-1, keepdims=True)).astype(BF16)
        key_grad += matmul(score_grad, query_rot, ((0,), (0,)))
        query_grad = factor * matmul(score_grad, key_rot, ((1,), (0,)))
        gain_part, query_low = head_backward(query_grad, gain_query, query_scale, query_hat, cosine, sine)
        query_gain += gain_part
        low_ref[..., columns] = query_low.reshape(block)
    key_gain, key_low = head_backward(factor * key_grad, gain_key, key_scale, key_hat, cosine, sine)
    low_ref[..., key_at:key_at + head_size] = key_low.reshape(block)
    low_ref[..., key_at + head_size:] = value_grad.astype(BF16).reshape(block)
    gain_grad_ref[...] = jnp.concatenate([query_gain, key_gain, jnp.zeros((6, head_size), F32)], axis=0)

def mlp_forward_kernel(*refs, count):
    chunk_refs = refs[:count]
    w_mlp_ref = refs[count]
    gate_ref, up_ref, hidden_ref, chunk_ref = refs[-4:]
    pair = pl.program_id(0)

    def hold(at):
        chunk_ref[0] = chunk_refs[2 * at][...]
        chunk_ref[1] = chunk_refs[2 * at + 1][...]
    for at in range(count // 2):
        pl.when((pl.program_id(1) == 0) & (pair == at))(functools.partial(hold, at))
    chunk = chunk_ref[...].reshape(-1, chunk_ref.shape[-1])
    half = w_mlp_ref.shape[1] // 2
    gate = matmul(chunk, w_mlp_ref[:, :half], ((1,), (0,)))
    up = matmul(chunk, w_mlp_ref[:, half:], ((1,), (0,)))
    gate_ref[...] = gate.reshape(gate_ref.shape)
    up_ref[...] = up.reshape(gate_ref.shape)
    hidden_ref[...] = (gate * jax.nn.sigmoid(gate) * up).astype(BF16).reshape(gate_ref.shape)

def mlp_forward(base, chunks, w_mlp, params, cost, *kept):
    count = len(chunks)
    rows, width = chunks[0].shape
    columns = w_mlp.shape[1] // 2
    step = columns
    shape = (8, rows, columns)
    out_spec = pl.BlockSpec((2, rows, step), lambda i, j: (base + i, 0, j))
    return pl.pallas_call(functools.partial(mlp_forward_kernel, count=count), grid=(count // 2, columns // step), in_specs=[pl.BlockSpec((rows, width), lambda i, j: (0, 0))] * count + [pl.BlockSpec(memory_space=pltpu.VMEM)] + [pl.BlockSpec(memory_space=pl.ANY)] * len(kept), out_specs=(out_spec,) * 3 + (pl.BlockSpec((2, rows, width), lambda i, j: (base + i, 0, 0)),), out_shape=(jax.ShapeDtypeStruct(shape, F32), jax.ShapeDtypeStruct(shape, F32), jax.ShapeDtypeStruct(shape, BF16), jax.ShapeDtypeStruct((8, rows, width), BF16)), input_output_aliases={count + 1 + at: at for at in range(len(kept))}, compiler_params=params, cost_estimate=cost)(*chunks, w_mlp, *kept)

def chunk_grad_kernel(left_ref, *refs):
    *chunk_refs, out_ref = refs
    total = 0.0
    for at, chunk_ref in enumerate(chunk_refs):
        total += matmul(left_ref[at], chunk_ref[...], ((0,), (0,)))
    out_ref[...] = total.astype(BF16)

def chunk_grad(left, chunks, params, cost):
    count, rows, columns = left.shape
    width = chunks[0].shape[1]
    step = 512
    return pl.pallas_call(chunk_grad_kernel, grid=(width // step,), in_specs=[pl.BlockSpec(left.shape, lambda j: (0, 0, 0))] + [pl.BlockSpec((rows, step), lambda j: (0, j))] * count, out_specs=pl.BlockSpec((columns, step), lambda j: (0, j)), out_shape=jax.ShapeDtypeStruct((columns, width), BF16), compiler_params=params, cost_estimate=cost)(left, *chunks)

def mlp_backward_kernel(gate_ref, up_ref, w_down_ref, w_mlp_ref, *refs, count):
    cotangent_refs = refs[:count]
    held_ref = refs[-1]
    grad_ref = refs[-count - 2]
    second_refs = refs[-count - 1:-1]
    pair, rows, columns = gate_ref.shape

    def hold(at):
        held_ref[:rows] = cotangent_refs[at][...]
        held_ref[rows:] = cotangent_refs[at + 1][...]
    for at in range(0, count, 2):
        pl.when(pl.program_id(0) == at // 2)(functools.partial(hold, at))
    cotangent = held_ref[...]
    hidden_grad = matmul(cotangent, w_down_ref[...], ((1,), (1,)))
    gate = gate_ref[...].reshape(pair * rows, -1)
    up = up_ref[...].reshape(pair * rows, -1)
    sigma = jax.nn.sigmoid(gate)
    gate_grad = hidden_grad * up * sigma * (1.0 + gate * (1.0 - sigma))
    up_grad = hidden_grad * gate * sigma
    grad = jnp.concatenate([gate_grad.astype(BF16), up_grad.astype(BF16)], axis=1)
    grad_ref[...] = grad.reshape(grad_ref.shape)
    second = matmul(grad, w_mlp_ref[...], ((1,), (1,))).astype(BF16)

    def store(at):
        second_refs[at][...] = second[:rows]
        second_refs[at + 1][...] = second[rows:]
    for at in range(0, count, 2):
        pl.when(pl.program_id(0) == at // 2)(functools.partial(store, at))

def mlp_backward(base, chunks, operands, params, cost, *kept):
    gate = operands[0]
    count = len(chunks)
    rows, width = chunks[0].shape
    columns = gate.shape[-1]

    def pair_spec(last):
        return pl.BlockSpec((2, rows, last), lambda i: (base + i, 0, 0))
    whole = pl.BlockSpec((rows, width), lambda i: (0, 0))
    return pl.pallas_call(functools.partial(mlp_backward_kernel, count=count), grid=(count // 2,), in_specs=[pair_spec(columns)] * 2 + [pl.BlockSpec(memory_space=pltpu.VMEM)] * 2 + [whole] * count + [pl.BlockSpec(memory_space=pl.ANY)] * len(kept), out_specs=(pair_spec(2 * columns),) + (whole,) * count, out_shape=(jax.ShapeDtypeStruct((8, rows, 2 * columns), BF16),) + (jax.ShapeDtypeStruct((rows, width), BF16),) * count, scratch_shapes=[pltpu.VMEM((2 * rows, width), BF16)], input_output_aliases={4 + count + at: at for at in range(len(kept))}, compiler_params=params, cost_estimate=cost)(*operands, *chunks, *kept)

def as_row(column):
    rows = column.shape[0]
    row = lax.broadcasted_iota(jnp.int32, (rows, rows), 0)
    place = lax.broadcasted_iota(jnp.int32, (rows, rows), 1)
    return jnp.sum(jnp.where(row == place, column, 0.0), axis=0, keepdims=True)

def pack_kernel(gate_ref, up_ref, out_ref, *, step):
    plane, _, columns = out_ref.shape
    hidden = columns // 2
    for g in range(plane):
        for at, ref in enumerate((gate_ref, up_ref)):
            parts = [ref[:, start + g * step:start + (g + 1) * step] for start in range(0, ref.shape[1], plane * step)]
            out_ref[g, :, at * hidden:(at + 1) * hidden] = jnp.concatenate(parts, axis=1)

def unpack_kernel(back_ref, gate_ref, up_ref, gain_ref, gate_out, up_out, gain_out, *, step):
    plane, _, columns = back_ref.shape
    hidden = columns // 2
    total = 0.0
    for at, (weight_ref, out_ref) in enumerate(((gate_ref, gate_out), (up_ref, up_out))):
        parts = [back_ref[g, :, at * hidden + start:at * hidden + start + step] for start in range(0, hidden, step) for g in range(plane)]
        grad = jnp.concatenate(parts, axis=1).astype(F32)
        out_ref[...] = grad
        total += jnp.sum(grad * weight_ref[...].astype(F32), axis=1, keepdims=True)
    gain_out[...] = as_row(total / gain_ref[...])

def attn_unpack_kernel(back_ref, *refs):
    weight_refs, gain_ref = (refs[:3], refs[3])
    out_refs, gain_out, line_out = (refs[4:7], refs[7], refs[8])
    plane = back_ref.shape[0]
    rows = gain_ref.shape[0]
    lines, total = (0.0, 0.0)
    for g in range(plane):
        back = back_ref[g].astype(F32)
        lines += back[rows:]
        at = 0
        for weight_ref, out_ref in zip(weight_refs, out_refs, strict=True):
            step = weight_ref.shape[1] // plane
            grad = back[:rows, at:at + step]
            columns = slice(g * step, (g + 1) * step)
            out_ref[:, columns] = grad
            total += jnp.sum(grad * weight_ref[:, columns].astype(F32), axis=1, keepdims=True)
            at += step
    gain_out[...] = as_row(total / gain_ref[...])
    line_out[...] = lines

def shards(tokens, segments, cotangent, w_query, key_projection_weight, value_projection_weight, w_output, w_gate, w_up, w_down, gain_attn, gain_query, gain_key, gain_mlp):
    outer = lax.axis_size('outer')
    plane = lax.axis_size('inner') * lax.axis_size('seq')
    local_sequences, local_rows, width = tokens.shape
    total_rows = segments.shape[1]
    rows_here = local_sequences * local_rows
    weight_rows = w_query.shape[0]
    head_size = gain_query.shape[0] * outer * plane
    query_columns = w_query.shape[1] // plane
    key_columns = key_projection_weight.shape[1] // plane
    attn_columns = query_columns + 2 * key_columns
    hidden_rows = w_down.shape[0]
    hidden_columns = hidden_rows * outer
    routes = plane_routes(outer)
    seq_index = lax.axis_index('seq')
    first_core = seq_index % 2 == 0
    tokens_flat = tokens.reshape(rows_here, width)
    segments_there = lax.ppermute(segments, EVERY, routes[3])
    tokens_near = ()
    segments_two = jnp.stack([segments, segments_there])
    core, row = (seq_index % 2, seq_index // 2)
    offsets = jnp.stack([(row ^ r) * 2 + (core ^ c) for r in range(2) for c in range(2)])
    token_index = (offsets[:, None] * local_rows + jnp.arange(local_rows, dtype=jnp.int32)[None]).reshape(-1)
    segments_here = jnp.take(segments_two, token_index, axis=2)
    doc_start = jnp.sum((segments_two[:, :, None, :] < segments_here[:, :, :, None]).astype(jnp.int32), axis=-1)
    positions = (token_index - doc_start).astype(F32)
    half_size = head_size // 2
    frequency = jnp.power(THETA, -(jnp.arange(half_size, dtype=F32) * 2.0 / head_size))
    angles = positions[..., None] * frequency
    cosine, sine = (jnp.cos(angles), jnp.sin(angles))
    cosine = jnp.concatenate([cosine, cosine], axis=-1)
    sine = jnp.concatenate([-sine, sine], axis=-1)
    start_table = doc_start[..., None]
    index_col = token_index[:, None]
    index_row = token_index[None, :]

    def by_column(values):
        return values.reshape(values.shape[0], plane, -1).transpose(1, 0, 2)
    gain_rows = 8
    gain_count = gain_query.shape[0]
    gain_line = jnp.concatenate([gain_attn, gain_mlp, gain_query, gain_key])
    gain_line = jnp.pad(gain_line[None], ((0, gain_rows - 1), (0, attn_columns - gain_line.shape[0])))
    head_pairs = head_route(outer, plane)
    output_rows = lax.all_gather(w_output, 'outer', axis=0)
    attn_send = jnp.concatenate([by_column(w_query), by_column(key_projection_weight), by_column(value_projection_weight)], axis=-1)
    attn_send = jnp.concatenate([attn_send, jnp.broadcast_to(gain_line, (plane,) + gain_line.shape)], axis=1)
    attn_part = lax.all_to_all(attn_send, PLANE, 0, 0, tiled=True)
    ties = ()
    if 0 in (1, 3):
        ties += (output_rows,)
    if 0 in (2, 3):
        ties += tuple(tokens_near)
    attn_full = lax.all_gather(after(attn_part, *ties), 'outer', axis=0, tiled=True)
    gain_lines = attn_full[:, weight_rows]
    at = 0
    gains = []
    for count in (weight_rows, weight_rows, gain_count, gain_count):
        gains.append(gain_lines[:, at:at + count].reshape(-1).astype(F32))
        at += count
    gain_attn_all, gain_mlp_all, gain_query_all, gain_key_all = gains
    head_gains = jnp.concatenate([gain_query_all[None], gain_key_all[None], jnp.zeros((6, head_size), F32)], axis=0)
    params = pltpu.CompilerParams(vmem_limit_bytes=VMEM_LIMIT)
    mlp_send = pl.pallas_call(functools.partial(pack_kernel, step=hidden_rows), out_shape=jax.ShapeDtypeStruct((plane, weight_rows, 2 * hidden_columns), BF16), compiler_params=params, cost_estimate=US(0))(w_gate, w_up)
    w_out = heads_gather(output_rows, query_columns)
    mlp_ties = ()
    mlp_part = lax.all_to_all(after(mlp_send, attn_part, *mlp_ties), PLANE, 0, 0, tiled=True)
    tokens_all, tokens_near = plane_gather(after(tokens_flat, mlp_part), routes, first_core)
    w_mlp = lax.all_gather(mlp_part.reshape(plane * weight_rows, 2 * hidden_columns), 'outer', axis=0, tiled=True)
    blocks = (2, 2, 2, local_sequences, local_rows)
    tables = (cosine, sine, start_table, index_col, index_row, head_gains)

    def whole_spec(value):
        return pl.BlockSpec(value.shape, lambda *at: (0,) * len(value.shape))

    def specs_of(side):
        def token_spec(columns):
            return pl.BlockSpec((None, 2, 2, None, local_rows, columns), lambda *at: (side, 0, 0, at[-1], 0, 0))

        def table_spec(rows, columns):
            return pl.BlockSpec((None, None, rows, columns), lambda *at: (side, at[-1], 0, 0))
        return (token_spec, table_spec, [table_spec(total_rows, head_size), table_spec(total_rows, head_size), table_spec(total_rows, 1), whole_spec(index_col), whole_spec(index_row), whole_spec(head_gains)])
    chunk_spec = pl.BlockSpec((local_rows, width), lambda *at: (at[-1], 0))

    def attention_forward(side, cost, chunks, weight, *kept):
        token_spec, _, table_specs = specs_of(side)
        operands = (*chunks, gain_attn_all[None], weight, w_out) + tables
        clean = (jax.ShapeDtypeStruct((width, attn_columns), BF16),) * (weight.ndim == 3)
        return pl.pallas_call(attention_kernel, grid=(local_sequences,), in_specs=[chunk_spec] * 4 + [pl.BlockSpec((1, width), lambda *at: (0, 0)), whole_spec(weight), whole_spec(w_out)] + table_specs + [pl.BlockSpec(memory_space=pl.ANY)] * len(kept), out_specs=(token_spec(width), token_spec(attn_columns), token_spec(query_columns)) + (chunk_spec,) * 4 + tuple((whole_spec(value) for value in clean)), out_shape=(jax.ShapeDtypeStruct(blocks + (width,), BF16), jax.ShapeDtypeStruct(blocks + (attn_columns,), F32), jax.ShapeDtypeStruct(blocks + (query_columns,), BF16)) + (jax.ShapeDtypeStruct((rows_here, width), BF16),) * 4 + clean, input_output_aliases={len(operands) + at: at for at in range(len(kept))}, compiler_params=params, cost_estimate=cost)(*operands, *kept)

    def attention_backward(side, cost, chunks, *kept):
        token_spec, table_spec, table_specs = specs_of(side)
        operands = (*chunks, projected, w_out) + tables
        return pl.pallas_call(attention_back_kernel, grid=(local_sequences,), in_specs=[chunk_spec] * 4 + [token_spec(attn_columns), whole_spec(w_out)] + table_specs + [pl.BlockSpec(memory_space=pl.ANY)] * len(kept), out_specs=(token_spec(attn_columns), pl.BlockSpec((None, 8, head_size), lambda *at: (at[-1], 0, 0))), out_shape=(jax.ShapeDtypeStruct(blocks + (attn_columns,), BF16), jax.ShapeDtypeStruct((local_sequences, 8, head_size), F32)), input_output_aliases={len(operands) + at: at for at in range(len(kept))}, compiler_params=params, cost_estimate=cost)(*operands, *kept)
    cotangent_flat = cotangent.reshape(rows_here, width)
    cotangent_all, cotangent_near = plane_gather(after(cotangent_flat, w_out, mlp_part, *tokens_all), routes, first_core)
    tokens_all = after(tuple(tokens_all), mlp_part)
    *kept, there_0, there_1, there_2, there_3, w_attn = attention_forward(1, US(0), tokens_all[4:], attn_full)
    scatter = Scatter(routes, first_core)
    far_sum = scatter.far(there_2, there_3)
    inner_sum = scatter.inner(there_0, there_1)
    tokens_own = after(tokens_all, *cotangent_near)
    *kept, here_0, here_1, here_2, here_3 = attention_forward(0, US(14), tokens_own[:4], w_attn, *kept)
    scatter.row(here_2, after(here_3, scatter.from_far))
    scatter.near()
    normed, projected, mixed = kept
    normed = normed.reshape(-1, width)
    mixed = mixed.reshape(-1, query_columns)
    w_down_here = lax.all_gather(after(w_down, mixed), 'outer', axis=0, tiled=True)
    tokens_here = tokens_flat.astype(F32)
    middle = tokens_here + scatter.own(here_0, here_1)
    scale_two = rms_scale(middle)
    hat_two = middle * scale_two
    normed_two, _ = plane_gather((hat_two * gain_mlp_all).astype(BF16), routes, first_core)
    mlp_params = pltpu.CompilerParams(vmem_limit_bytes=MLP_VMEM_LIMIT)
    gate, up, hidden, normed_two = mlp_forward(0, normed_two, w_mlp, mlp_params, US(0))
    normed_two = normed_two.reshape(-1, width)

    def weight_grad(left, right):
        return lax.dot_general(left, right, (((0,), (0,)), ((), ())), preferred_element_type=F32).astype(BF16)

    def times_transposed(left, right):
        return lax.dot_general(left, right, (((1,), (1,)), ((), ())), preferred_element_type=F32)

    def sum_planes(values):
        return lax.psum_scatter(values, 'outer', scatter_dimension=0, tiled=True)
    down_grad = chunk_grad(hidden, cotangent_all, mlp_params, US(6))
    down_sum = sum_planes(down_grad)
    operands = (after(gate, down_grad), up, w_down_here, w_mlp)
    scatter = Scatter(routes, first_core)
    mlp_grad, *far = mlp_backward(3, cotangent_all[6:], operands, mlp_params, US(0))
    far_sum = scatter.far(*far)
    mlp_grad = after(mlp_grad, far_sum)
    mlp_grad, *near = mlp_backward(1, cotangent_all[2:6], operands, mlp_params, US(14), mlp_grad)
    near = after(tuple(near), scatter.from_far)
    scatter.row(*near[:2])
    scatter.inner(*near[2:])
    near_sums = scatter.near()
    mlp_grad, *own = mlp_backward(0, cotangent_all[:2], operands, mlp_params, US(14), mlp_grad)
    mlp_grad = mlp_grad.reshape(-1, 2 * hidden_columns)
    mlp_tie = normed_two
    mlp_tie = after(mlp_tie, near_sums[1])
    mlp_part_grad = weight_grad(mlp_tie, mlp_grad)
    mlp_wgrad = sum_planes(after(mlp_part_grad, down_sum))
    down_out = jnp.dot(after(hidden, *own).reshape(-1, hidden_columns), w_down_here, preferred_element_type=F32).astype(BF16)
    second_grad = scatter.own(*own)
    middle_grad = cotangent_flat.astype(F32) + norm_back(after(second_grad, mlp_part_grad) * gain_mlp_all, hat_two, scale_two)
    out_blocks, _ = plane_gather(middle_grad.astype(BF16), routes, first_core)
    output, output_far, output_near = plane_scatter(after(down_out, out_blocks[6]).reshape(plane, rows_here, width), routes, first_core)
    output = middle + output
    mixed_chunks = mixed.reshape(plane, rows_here, query_columns)
    low, gain_here = attention_backward(0, US(14), out_blocks[:4])
    low, gain_there = attention_backward(1, US(14), out_blocks[4:], low)
    low = low.reshape(-1, attn_columns)
    low = after(low, output_far)
    normed_grad = times_transposed(low, w_attn).astype(BF16)
    low = after(low, normed_grad)
    head_gain_grad = jnp.sum(gain_here + gain_there, axis=0)[:2].reshape(-1)
    gain_lines = jnp.zeros((outer, gain_rows, attn_columns), BF16)
    gain_lines = gain_lines.at[:, 0, :2 * head_size].set(jnp.broadcast_to(head_gain_grad.astype(BF16), (outer, 2 * head_size)))
    attn_wgrad = jnp.concatenate([weight_grad(normed, low).reshape(outer, -1, attn_columns), gain_lines], axis=1)
    mlp_back = lax.all_to_all(mlp_wgrad.reshape(plane, weight_rows, 2 * hidden_columns), PLANE, 0, 0, tiled=True)
    normed_low = low
    if 3 in (1, 2):
        normed_low = after(normed_low, attn_wgrad)
    output_wgrad = chunk_grad(after(mixed_chunks, normed_grad, attn_wgrad), out_blocks, params, US(0))
    output_local = output_wgrad
    attn_flat = after(attn_wgrad.reshape(-1, attn_columns), mlp_wgrad)
    attn_wgrad = sum_planes(attn_flat)
    output_wgrad = sum_planes(after(output_wgrad, attn_wgrad))

    def unpack_mlp(mlp_back):
        return pl.pallas_call(functools.partial(unpack_kernel, step=hidden_rows), out_shape=(jax.ShapeDtypeStruct(w_gate.shape, F32), jax.ShapeDtypeStruct(w_up.shape, F32), jax.ShapeDtypeStruct((1, weight_rows), F32)), compiler_params=params, cost_estimate=US(0))(mlp_back, w_gate, w_up, gain_mlp.astype(F32)[:, None])
    normed_grad = plane_scatter(after(normed_grad, output_near).reshape(plane, rows_here, width), routes, first_core, attn_wgrad, far_needed=())[0]
    attn_rows = attn_wgrad[:plane * weight_rows].reshape(plane, weight_rows, attn_columns)
    gain_send = jnp.broadcast_to(attn_wgrad[plane * weight_rows:], (plane, gain_rows, attn_columns))
    attn_send = jnp.concatenate([attn_rows, gain_send], axis=1)
    attn_back = lax.all_to_all(attn_send, PLANE, 0, 0, tiled=True)
    scale_one = rms_scale(tokens_here)
    input_grad = middle_grad + norm_back(after(normed_grad, attn_back) * gain_attn_all, tokens_here * scale_one, scale_one)
    mlp_back = after(mlp_back, attn_back)
    gate_sum, up_sum, mlp_gain_sum = unpack_mlp(mlp_back)
    attn_back = after(attn_back, output_wgrad)
    query_sum, key_sum, value_sum, attn_gain_sum, head_gain_sum = pl.pallas_call(attn_unpack_kernel, out_shape=(jax.ShapeDtypeStruct(w_query.shape, F32), jax.ShapeDtypeStruct(key_projection_weight.shape, F32), jax.ShapeDtypeStruct(value_projection_weight.shape, F32), jax.ShapeDtypeStruct((1, weight_rows), F32), jax.ShapeDtypeStruct((gain_rows, attn_columns), F32)), compiler_params=params, cost_estimate=CHEAP)(attn_back, w_query, key_projection_weight, value_projection_weight, gain_attn.astype(F32)[:, None])
    output_sum = lax.ppermute(output_wgrad, EVERY, [(target, source) for source, target in head_pairs]).astype(F32)
    place = lax.axis_index(EVERY) * gain_count
    query_gain_sum = lax.dynamic_slice_in_dim(head_gain_sum[0], place, gain_count)
    key_gain_sum = lax.dynamic_slice_in_dim(head_gain_sum[0], head_size + place, gain_count)
    return (output.astype(BF16).reshape(tokens.shape), input_grad.astype(BF16).reshape(tokens.shape), query_sum, key_sum, value_sum, output_sum, gate_sum, up_sum, down_sum.astype(F32), attn_gain_sum[0], query_gain_sum, key_gain_sum, mlp_gain_sum[0])

def solution(mesh):
    seq = mesh.shape['seq']
    split = Mesh(mesh.devices.reshape(-1, 2, seq), EVERY)
    rows = P(('outer', 'inner'), 'seq', None)
    weight = P(EVERY, None)
    gain = P(EVERY)
    return jax.shard_map(shards, mesh=split, in_specs=(rows, P(('outer', 'inner'), None), rows) + (weight,) * 7 + (gain,) * 4, out_specs=(rows, rows) + (weight,) * 7 + (gain,) * 4, check_vma=False)
```
